32 devices in a mesh: sp: 16 (over z, x, core), hd: 2 (over y).
Axes of the slice: x: 2, y: 2, z: 4, core: 2. Of those that a mesh axis runs over, the one named last changes fastest.
Arguments:
- stream: bfloat16 [3, 2, 16, 5120], P(None, 'hd', 'sp'), may hold values from -6 to 6
- queries: bfloat16 [3, 2, 16, 5120], P(None, None, 'sp', 'hd'), may hold values from -40 to 40
- span_k: bfloat16 [3, 2, 16, 5120], P(None, None, 'sp', 'hd'), may hold values from -40 to 40
- span_v: bfloat16 [3, 2, 16, 5120], P(None, None, 'sp', 'hd'), may hold values from -6 to 6
- cache_k: bfloat16 [1536, 5120], P('sp', 'hd'), may hold values from -6 to 6
- cache_v: bfloat16 [1536, 5120], P('sp', 'hd'), may hold values from -6 to 6
- cache_age: int32 [1536], P('sp'), may hold values from 0 to 20, as said below
- history: int32 [1], replicated, may hold values from 1 to 20
- out_weight: bfloat16 [5120, 5120], P('hd', 'sp'), may hold values from -2 to 2
- attn_gate: float32 [5120], replicated, may hold values from 0.5 to 1.5
- head_shift: float32 [5120], replicated, may hold values from -3 to 3
- head_scale: float32 [5120], replicated, may hold values from -1.75 to 1.75
- head_weight: bfloat16 [5120, 64], replicated, may hold values from -0.078125 to 0.078125
- latent_cache: bfloat16 [2, 4, 32, 16], P(None, 'hd', 'sp'), may hold values from -6 to 6
- conv_weight: bfloat16 [432, 384], replicated, may hold values from -0.3125 to 0.3125
- rms_gain: float32 [384], replicated, may hold values from 0.25 to 1.75
Outputs:
- stream_out: bfloat16 [3, 2, 16, 5120], P(None, 'hd', 'sp')
- decoded: bfloat16 [3, 4, 32, 384], P(None, 'hd', 'sp')
The draws below stay inside these ranges and needn't reach their ends.
Inputs may be any that keep to these rules, and one draw needn't show every extreme that they name: `cache_age`: 20 marks an empty cache slot. Among the 96 slots of each index of sp the live ones come first and number at least 24; some index of sp has all its slots live.
All inputs are finite; a program needn't handle non-finite values.
Results may differ from the reference program's by a relative error of at most 0.017.
Values may be sent and summed in bfloat16 or wider, within the bound.
A program may use at most 64 MiB of HBM per device.

```python
import math
import jax
import jax.numpy as jnp
from jax import lax

D = 5120
HEADS = 40
HDIM = 128
LAT = 16
CHAN = 384
PATCH = 2
FRAMES = 3
MAXH = 20
CSLOT = 96
HT = 2
WT = 16
CROWS = 1536
LH = 4
LW = 32


def drawn_pair(key):
    base_key = jax.random.fold_in(key, 7177)
    key_q, key_k = jax.random.split(base_key, 2)
    full_shape = (FRAMES, HT, WT, D)
    query_base = 1.4 * jax.random.truncated_normal(key_q, -4.0, 4.0, full_shape, jnp.float32)
    key_base = jax.random.truncated_normal(key_k, -4.0, 4.0, full_shape, jnp.float32)
    return (query_base, key_base)


def draw_queries(key, part):
    return drawn_pair(key)[0].astype(jnp.bfloat16)


def draw_span_k(key, part):
    return drawn_pair(key)[1].astype(jnp.bfloat16)


def draw_cache_age(key, part):
    key_live, key_full, key_age = jax.random.split(jax.random.fold_in(key, 3301), 3)
    groups = CROWS // CSLOT
    live_count = jax.random.randint(key_live, (groups,), CSLOT // 4, CSLOT + 1)
    full_device = jax.random.randint(key_full, (), 0, groups)
    live_count = jnp.where(jnp.arange(groups) == full_device, CSLOT, live_count)
    age_draw = jax.random.randint(key_age, (CROWS,), 0, MAXH)
    slot_pos = jnp.arange(CROWS) % CSLOT
    owner_row = jnp.arange(CROWS) // CSLOT
    return jnp.where(slot_pos < live_count[owner_row], age_draw, MAXH).astype(jnp.int32)


def levels(rng, dims, cuts, smallest, high):
    level = 1.0
    for axis_at, shards_of in cuts:
        steps = jax.random.uniform(jax.random.fold_in(jax.random.fold_in(rng, 6), axis_at), (shards_of,), jnp.float32, smallest / len(cuts), high / len(cuts))
        level = level * jnp.repeat(jnp.exp(steps), dims[axis_at] // shards_of).reshape((-1,) + (1,) * (len(dims) - 1 - axis_at))
    return level


def scatter_about(rng, shape, scale, reach, cuts=(), dtype=jnp.bfloat16):
    factor_of = levels(rng, shape, cuts, -0.22, 0.18) if cuts else 1.0
    drawn = jax.random.normal(rng, shape, jnp.float32) * scale * factor_of
    return jnp.minimum(jnp.maximum(drawn, -reach), reach).astype(dtype)


def setup_inputs(seed: int = 0) -> dict:
    key_list = jax.random.split(jax.random.key(seed), 17)
    stream = scatter_about(key_list[0], (FRAMES, HT, WT, D), 1.0, 6.0, ((1, 2), (2, 16)))
    queries = draw_queries(jax.random.fold_in(key_list[16], 71), 0)
    span_k = draw_span_k(jax.random.fold_in(key_list[16], 71), 0)
    span_v = scatter_about(key_list[3], (FRAMES, HT, WT, D), 1.0, 6.0, ((2, 16), (3, 2)))
    cache_k = scatter_about(key_list[4], (CROWS, D), 1.0, 6.0, ((0, 16), (1, 2)))
    cache_v = scatter_about(key_list[5], (CROWS, D), 1.0, 6.0, ((0, 16), (1, 2)))
    cache_age = draw_cache_age(jax.random.fold_in(key_list[16], 71), 0)
    history = jax.random.randint(key_list[7], (1,), 1, MAXH + 1).astype(jnp.int32)
    out_weight = scatter_about(key_list[8], (D, D), (max(HDIM // 16, 1)) ** -0.5, 2.0, ((0, 2), (1, 16)))
    attn_gate = jnp.clip(jax.random.uniform(key_list[9], (D,), jnp.float32, 0.5, 1.5), 0.5, 1.5)
    head_shift = scatter_about(key_list[10], (D,), 0.5, 3.0, (), jnp.float32)
    head_scale = scatter_about(key_list[11], (D,), 0.3, 1.75, (), jnp.float32)
    head_weight = scatter_about(key_list[12], (D, PATCH * PATCH * LAT), D ** -0.5, 0.078125)
    latent_cache = scatter_about(key_list[13], (2, LH, LW, LAT), 1.0, 6.0, ((1, 2), (2, 16)))
    conv_weight = scatter_about(key_list[14], (27 * LAT, CHAN), (27 * LAT) ** -0.5, 0.3125)
    rms_gain = jnp.clip(1.0 + 0.15 * jax.random.normal(key_list[15], (CHAN,), jnp.float32), 0.25, 1.75)
    return dict(stream=stream, queries=queries, span_k=span_k, span_v=span_v, cache_k=cache_k, cache_v=cache_v, cache_age=cache_age, history=history, out_weight=out_weight, attn_gate=attn_gate, head_shift=head_shift, head_scale=head_scale, head_weight=head_weight, latent_cache=latent_cache, conv_weight=conv_weight, rms_gain=rms_gain)


def causal_conv(padded, frames, height, breadth, conv_weight, rms_gain):
    tap_list = []
    for step_t in range(3):
        for step_i in range(3):
            for step_j in range(3):
                tap_list.append(padded[step_t:step_t + frames, step_i:step_i + height, step_j:step_j + breadth, :])
    patches = jnp.concatenate(tap_list, axis=-1)
    conv_out = jnp.dot(patches.reshape(-1, patches.shape[-1]), conv_weight, preferred_element_type=jnp.float32)
    mean_square = lax.optimization_barrier(jnp.mean(conv_out * conv_out, axis=-1, keepdims=True))
    scaled = conv_out * lax.rsqrt(mean_square + 1e-06) * rms_gain
    return jax.nn.silu(scaled).astype(jnp.bfloat16).reshape(frames, height, breadth, -1)

def reference(stream, queries, span_k, span_v, cache_k, cache_v, cache_age, history, out_weight, attn_gate, head_shift, head_scale, head_weight, latent_cache, conv_weight, rms_gain):
    query_count = FRAMES * HT * WT
    factor = 1.0 / math.sqrt(HDIM)
    query_all = queries.reshape(query_count, HEADS, HDIM).astype(jnp.float32)
    group_ck = cache_k.reshape(WT, CSLOT, D)
    group_cv = cache_v.reshape(WT, CSLOT, D)
    group_age = cache_age.reshape(WT, CSLOT)
    group_nk = jnp.transpose(span_k, (2, 0, 1, 3)).reshape(WT, FRAMES * HT, D)
    group_nv = jnp.transpose(span_v, (2, 0, 1, 3)).reshape(WT, FRAMES * HT, D)

    def group_step(carry, group):
        run_top, run_total, run_out = carry
        cache_keys, cache_vals, slot_age, new_keys, new_vals = group
        key_all = jnp.concatenate([cache_keys, new_keys], axis=0).reshape(-1, HEADS, HDIM).astype(jnp.float32)
        val_all = jnp.concatenate([cache_vals, new_vals], axis=0).reshape(-1, HEADS, HDIM).astype(jnp.float32)
        is_valid = jnp.concatenate([slot_age < history[0], jnp.ones((FRAMES * HT,), jnp.bool_)])
        scores = jnp.einsum('qhd,khd->hqk', query_all, key_all) * factor
        scores = jnp.where(is_valid[None, None, :], scores, -1e+30)
        group_max = lax.optimization_barrier(jnp.max(scores, axis=2))
        rounded = lax.optimization_barrier(jnp.exp(scores - group_max[:, :, None]).astype(jnp.bfloat16))
        weights = rounded.astype(jnp.float32)
        group_total = lax.optimization_barrier(jnp.sum(weights, axis=2))
        group_out = jnp.einsum('hqk,khd->hqd', weights, val_all)
        new_top = jnp.maximum(run_top, group_max)
        old_w = jnp.exp(run_top - new_top)
        new_w = jnp.exp(group_max - new_top)
        return ((new_top, run_total * old_w + group_total * new_w, run_out * old_w[:, :, None] + group_out * new_w[:, :, None]), None)
    start_carry = (jnp.full((HEADS, query_count), -1e+30, jnp.float32), jnp.zeros((HEADS, query_count), jnp.float32), jnp.zeros((HEADS, query_count, HDIM), jnp.float32))
    final_carry, _ = lax.scan(group_step, start_carry, (group_ck, group_cv, group_age, group_nk, group_nv))
    attended_f = final_carry[2] / final_carry[1][:, :, None]
    attended = jnp.transpose(attended_f, (1, 0, 2)).reshape(query_count, D).astype(jnp.bfloat16)
    projected = jnp.dot(attended, out_weight, preferred_element_type=jnp.float32).reshape(FRAMES, HT, WT, D)
    stream_out = (stream.astype(jnp.float32) + attn_gate * projected).astype(jnp.bfloat16)
    mixed_f = stream_out.astype(jnp.float32)
    centre_mean = lax.optimization_barrier(jnp.mean(mixed_f, axis=-1, keepdims=True))
    centred = mixed_f - centre_mean
    variance = lax.optimization_barrier(jnp.mean(centred * centred, axis=-1, keepdims=True))
    normed = (centred * lax.rsqrt(variance + 1e-06) * (1.0 + head_scale) + head_shift).astype(jnp.bfloat16)
    patch_values = jnp.dot(normed.reshape(-1, D), head_weight, preferred_element_type=jnp.float32).astype(jnp.bfloat16)
    patch_values = patch_values.reshape(FRAMES, HT, WT, PATCH, PATCH, LAT)
    latent = jnp.transpose(patch_values, (0, 1, 3, 2, 4, 5)).reshape(FRAMES, HT * PATCH, WT * PATCH, LAT)
    sequence = jnp.concatenate([latent_cache, latent], axis=0)
    padded = jnp.pad(sequence, ((0, 0), (1, 1), (1, 1), (0, 0)))
    decoded = causal_conv(padded, FRAMES, HT * PATCH, WT * PATCH, conv_weight, rms_gain)
    return (stream_out, decoded)
```

```python
import functools
import math

import jax
import jax.numpy as jnp
import numpy as np
from jax import lax
from jax.experimental import pallas as pl
from jax.experimental.pallas import tpu as pltpu
from jax.sharding import PartitionSpec as P

HDIM = 128
LANES = 128
MESH = pl.DeviceIdType.MESH
F32 = jnp.float32
BF16 = jnp.bfloat16


def up(value, unit):
    return -(-value // unit) * unit


class Sizes:
    def __init__(self, mesh, queries, cache_k, out_weight):
        self.nsp, self.nhd = mesh.shape["sp"], mesh.shape["hd"]
        self.nchip = self.nsp // 2
        self.frames, self.rows, _, self.width = queries.shape
        self.heads = self.width // HDIM
        self.own = self.rows // self.nhd
        self.tokens = self.frames * self.rows
        self.slot = up(self.own * self.frames, 4)
        self.tp = self.slot * self.nhd
        self.halves = 2 if self.tp % 16 and self.heads % 2 == 0 else 1
        if self.halves == 1:
            self.tp = up(self.tp, 16)
        self.block = self.halves * self.tp
        self.lanes = self.width // self.halves
        self.pairs = self.heads // self.halves
        self.cache = cache_k.shape[0]
        self.span = up(self.tp, 16)
        self.keys = self.cache + self.span
        self.all = self.nsp * self.block
        self.part = out_weight.shape[1]
        self.pieces = -(-self.part // LANES)
        self.message = up(self.pieces * self.slot, 16)
        self.model = self.part * self.nsp

    def slots(self):
        for f in range(self.frames):
            for r in range(self.rows):
                yield (r // self.own) * self.slot + (r % self.own) * self.frames + f, f, r


def iota(shape, dim):
    return lax.broadcasted_iota(jnp.int32, shape, dim)


def merge_stats(stats):
    top = functools.reduce(jnp.maximum, stats)
    scales = [jnp.exp(s - top) for s in stats]
    total = functools.reduce(
        jnp.add, [s * pltpu.roll(a, 64, 1) for s, a in zip(stats, scales)]
    )
    return top, total, scales


def kernel(
    z, q_ref, k_ref, v_ref, valid_ref, stream_ref, gate_ref, shift_ref, scale_ref, latc_ref, gain_ref,
    ck_hbm, cv_hbm, w_hbm, hw_hbm, cw_hbm,
    so_ref, dec_ref,
    g, att, o, st, o_in, s_in, co, cs, o_got, s_got, k2, v2, w, hw, cw, zs, z_got, h, r_got, near, msg, tmp,
    local_sem, ag_send, ag_recv, fw_send, fw_recv, sib_send, sib_recv, b_send, b_recv,
    hd_send, hd_recv, e_send, e_recv, n_send, n_recv,
):
    me, my = lax.axis_index("sp"), lax.axis_index("hd")
    core, chip = me % 2, me // 2
    sib = me + 1 - 2 * core
    nchip, block = z.nchip, z.block

    def peer(k):
        return (chip + k) % nchip

    def source(k):
        return (chip + nchip - k) % nchip

    def rows_of(which_core, which_chip):
        return pl.ds(pl.multiple_of((which_core * nchip + which_chip) * block, block), block)

    def chip_rows(which_chip):
        return pl.ds(pl.multiple_of(which_chip * block, block), block)

    def remote(src, dst, ssem, rsem, sp, hd):
        return pltpu.make_async_remote_copy(
            src_ref=src, dst_ref=dst, send_sem=ssem, recv_sem=rsem,
            device_id=(sp, hd), device_id_type=MESH,
        )

    loads = []

    def load(src, dst):
        copy = pltpu.make_async_copy(src, dst, local_sem.at[len(loads)])
        copy.start()
        loads.append(copy)

    for half in range(z.halves):
        cols = pl.ds(half * z.lanes, z.lanes)
        load(ck_hbm.at[:, cols], k2.at[pl.ds(half * z.keys, z.cache)])
        load(cv_hbm.at[:, cols], v2.at[pl.ds(half * z.keys, z.cache)])
    attention_loads = len(loads)
    load(w_hbm, w)
    load(hw_hbm, hw)
    load(cw_hbm, cw)

    def packed(ref):
        row = iota((z.tp, z.width), 0)
        out = jnp.zeros((z.tp, z.width), F32)
        for slot, f, r in z.slots():
            out = jnp.where(row == slot, ref[f, r].astype(F32), out)
        return [out[:, i * z.lanes : (i + 1) * z.lanes] for i in range(z.halves)]

    g[rows_of(core, chip), :] = jnp.concatenate(packed(q_ref), axis=0).astype(BF16)
    near[...] = jnp.zeros_like(near)

    barrier = pltpu.get_barrier_semaphore()
    for k in range(1, z.nsp):
        pl.semaphore_signal(barrier, inc=1, device_id=((me + k) % z.nsp, my), device_id_type=MESH)
    for k in range(1, z.nhd):
        pl.semaphore_signal(barrier, inc=1, device_id=(me, (my + k) % z.nhd), device_id_type=MESH)

    def inside(dr, dc):
        ok = None
        for step, at, count in ((dr, my, z.nhd), (dc, me, z.nsp)):
            if step:
                here = (at + step >= 0) & (at + step < count)
                ok = here if ok is None else ok & here
        return ok

    greeted = z.nsp - 1 + z.nhd - 1
    for dr in (-1, 1):
        for dc in (-1, 1):

            @pl.when(inside(dr, dc))
            def _():
                pl.semaphore_signal(barrier, inc=1, device_id=(me + dc, my + dr), device_id_type=MESH)

            greeted = greeted + inside(dr, dc).astype(jnp.int32)
    pl.semaphore_wait(barrier, greeted)

    def gather_start(buf, phase):
        mine = rows_of(core, chip)
        first = [
            remote(buf.at[mine], buf.at[mine], ag_send.at[phase, k], ag_recv.at[phase, k],
                   peer(k) * 2 + core, my)
            for k in range(1, nchip)
        ]
        for copy in first:
            copy.start()
        return first

    def gather_finish(buf, phase, first):
        forwards = []
        for k in range(nchip):
            if k:
                first[k - 1].wait_recv()
            rows = rows_of(core, source(k))
            copy = remote(buf.at[rows], buf.at[rows], fw_send.at[phase, k], fw_recv.at[phase, k], sib, my)
            copy.start()
            forwards.append(copy)
        for copy in forwards:
            copy.wait_recv()
        return first + forwards

    first = gather_start(g, 0)
    for ref, buf in ((k_ref, k2), (v_ref, v2)):
        for half, part in enumerate(packed(ref)):
            if z.span > z.tp:
                part = jnp.concatenate([part, jnp.zeros((z.span - z.tp, z.lanes), F32)], axis=0)
            buf[pl.ds(half * z.keys + z.cache, z.span), :] = part.astype(BF16)
    for copy in loads[:attention_loads]:
        copy.wait()
    sent = gather_finish(g, 0, first)

    chunk = min(z.all, 256)
    total_keys = z.halves * z.keys
    lane = iota((chunk, LANES), 1)
    scale = 1.0 / math.sqrt(HDIM)
    mask = valid_ref[...] > 0.0
    if z.halves > 1:
        row_half = (iota((chunk, total_keys), 0) // z.tp) % z.halves
        col_half = (iota((chunk, total_keys), 1) >= z.keys).astype(jnp.int32)
        mask = mask & (row_half == col_half)
    else:
        mask = jnp.broadcast_to(mask, (chunk, total_keys))

    def attend(at, carry):
        rows = pl.ds(pl.multiple_of(at * chunk, chunk), chunk)
        stats = jnp.zeros((chunk, LANES), F32)
        for j in range(z.pairs):
            cols = pl.ds(j * HDIM, HDIM)
            scores = lax.dot_general(
                g[rows, cols], k2[:, cols], (((1,), (1,)), ((), ())), preferred_element_type=F32
            )
            scores = jnp.where(mask, scores * scale, -1e30)
            top = jnp.max(scores, axis=1, keepdims=True)
            weights = jnp.exp(scores - top).astype(BF16)
            total = jnp.sum(weights.astype(F32), axis=1, keepdims=True)
            out = jnp.dot(weights, v2[:, cols], preferred_element_type=F32)
            o[rows, cols] = out.astype(BF16)
            stats = jnp.where(lane == j, top, jnp.where(lane == j + 64, total, stats))
        st[rows, :] = stats
        return carry

    lax.fori_loop(0, z.all // chunk, attend, 0)

    half_rows = nchip * block
    theirs = pl.ds(pl.multiple_of((1 - core) * half_rows, half_rows), half_rows)
    pair = [
        remote(st.at[theirs], s_in, sib_send.at[0], sib_recv.at[0], sib, my),
        remote(o.at[theirs], o_in, sib_send.at[1], sib_recv.at[1], sib, my),
    ]
    for copy in pair:
        copy.start()
    for copy in sent:
        copy.wait_send()
    for copy in pair:
        copy.wait_recv()

    low = iota((block, LANES), 1) < 64
    exchanged = []
    for k in list(range(1, nchip)) + [0]:
        to = peer(k)
        mine, rows = rows_of(core, to), chip_rows(to)
        top, total, (a, b) = merge_stats([st[mine, :], s_in[rows, :]])
        cs[rows, :] = jnp.where(low, top, total)
        for j in range(z.pairs):
            cols = pl.ds(j * HDIM, HDIM)
            merged = (
                o[mine, cols].astype(F32) * a[:, j : j + 1]
                + o_in[rows, cols].astype(F32) * b[:, j : j + 1]
            )
            co[rows, cols] = merged.astype(BF16)
        if k:
            there = chip_rows(chip)
            for which, (src, dst) in enumerate(((cs, s_got), (co, o_got))):
                copy = remote(src.at[rows], dst.at[there], b_send.at[which, k], b_recv.at[which, k],
                              to * 2 + core, my)
                copy.start()
                exchanged.append(copy)
    own_rows = chip_rows(chip)
    s_got[own_rows, :] = cs[own_rows, :]
    o_got[own_rows, :] = co[own_rows, :]
    for copy in exchanged:
        copy.wait_recv()

    top, total, scales = merge_stats([s_got[pl.ds(i * block, block), :] for i in range(nchip)])
    inverse = pltpu.roll(1.0 / jnp.where(low, 1.0, total), 64, 1)
    for j in range(z.pairs):
        cols = pl.ds(j * HDIM, HDIM)
        summed = functools.reduce(
            jnp.add,
            [
                o_got[pl.ds(i * block, block), cols].astype(F32) * scales[i][:, j : j + 1]
                for i in range(nchip)
            ],
        )
        att[rows_of(core, chip), cols] = (summed * inverse[:, j : j + 1]).astype(BF16)

    first = gather_start(att, 1)
    for copy in pair + exchanged:
        copy.wait_send()
    for copy in loads[attention_loads:]:
        copy.wait()
    sent = gather_finish(att, 1, first)

    everything = att[...]
    proj = None
    for half in range(z.halves):
        term = jnp.dot(everything, w[pl.ds(half * z.lanes, z.lanes), :], preferred_element_type=F32)
        term = term.reshape(z.nsp, z.halves, z.tp, z.part)[:, half]
        proj = term if proj is None else proj + term
    proj = proj.reshape(z.nsp * z.tp, z.part).astype(BF16)
    out_rows, in_rows = z.nsp * z.message, z.nsp * z.tp
    out_at, in_at = iota((out_rows, in_rows), 0), iota((out_rows, in_rows), 1)
    out_sp, inner = out_at // z.message, out_at % z.message
    base = ((out_sp % 2) * nchip + out_sp // 2) * z.tp + inner % z.slot
    for owner in range(z.nhd):
        wanted = in_at == base + owner * z.slot
        cells = []
        moved = jnp.zeros((out_rows, LANES), F32)
        for piece in range(z.pieces):
            wide = min(LANES, z.part - piece * LANES)
            pick = jnp.where(wanted & (inner // z.slot == piece), 1.0, 0.0).astype(BF16)
            got = jnp.dot(pick, proj[:, piece * LANES : piece * LANES + wide], preferred_element_type=F32)
            if wide < LANES:
                got = jnp.concatenate([got, jnp.zeros((out_rows, LANES - wide), F32)], axis=1)
            moved = moved + got
        zs[owner] = moved.astype(BF16)

    swaps = []
    for k in range(1, z.nhd):
        to = (my + k) % z.nhd
        copy = remote(zs.at[to], z_got.at[my], hd_send.at[k], hd_recv.at[k], me, to)
        copy.start()
        swaps.append(copy)
    for copy in sent:
        copy.wait_send()
    summed = zs[my].astype(F32)
    for k in range(1, z.nhd):
        swaps[k - 1].wait_recv()
        summed = summed + z_got[(my + z.nhd - k) % z.nhd].astype(F32)
    h[...] = summed.astype(BF16)

    def message_rows(at):
        return pl.ds(pl.multiple_of(at * z.message, z.message), z.message)

    spread = []
    for k in range(1, z.nsp):
        to = (me + k) % z.nsp
        copy = remote(h.at[message_rows(to)], r_got.at[message_rows(me)], e_send.at[k], e_recv.at[k], to, my)
        copy.start()
        spread.append(copy)
    r_got[message_rows(me), :] = h[message_rows(me), :]
    for copy in swaps:
        copy.wait_send()
    for copy in spread:
        copy.wait_recv()

    got_all = r_got[...]
    to_rows, from_rows = z.nsp * 8, z.nsp * z.message
    to_at, from_at = iota((to_rows, from_rows), 0), iota((to_rows, from_rows), 1)
    by_piece = []
    for piece in range(z.pieces):
        pick = (from_at == (to_at // 8) * z.message + piece * z.slot + to_at % 8) & (to_at % 8 < z.slot)
        by_piece.append(jnp.dot(jnp.where(pick, 1.0, 0.0).astype(BF16), got_all, preferred_element_type=F32))
    lane8 = iota((8, LANES), 1)
    row8 = iota((8, LANES), 0)
    tiles = []
    for tile in range(z.model // LANES):
        value = jnp.zeros((8, LANES), F32)
        begin = tile * LANES
        for s in range(begin // z.part, (begin + LANES - 1) // z.part + 1):
            for piece in range(z.pieces):
                low_at = s * z.part + piece * LANES
                high_at = min(low_at + LANES, (s + 1) * z.part)
                a, b = max(low_at, begin), min(high_at, begin + LANES)
                if a >= b:
                    continue
                cell = by_piece[piece][s * 8 : (s + 1) * 8]
                if (low_at - begin) % LANES:
                    cell = pltpu.roll(cell, (low_at - begin) % LANES, 1)
                value = jnp.where((lane8 >= a - begin) & (lane8 < b - begin), cell, value)
        cols = pl.ds(begin, LANES)
        base_value = jnp.zeros((8, LANES), F32)
        for f in range(z.frames):
            base_value = jnp.where(row8 == f, stream_ref[f, :, cols].astype(F32), base_value)
        value = base_value + gate_ref[:, cols] * value
        value = value.astype(BF16).astype(F32)
        so_ref[:, cols] = value
        tiles.append(value)
    mean = jnp.sum(functools.reduce(jnp.add, tiles), axis=1, keepdims=True) / z.model
    centred = [t - mean for t in tiles]
    variance = jnp.sum(functools.reduce(jnp.add, [t * t for t in centred]), axis=1, keepdims=True) / z.model
    root = lax.rsqrt(variance + 1e-6)
    normed = []
    for tile, t in enumerate(centred):
        cols = pl.ds(tile * LANES, LANES)
        normed.append(t * root * (1.0 + scale_ref[:, cols]) + shift_ref[:, cols])
    normed = jnp.concatenate(normed, axis=1)
    normed = jnp.concatenate([normed, jnp.zeros_like(normed)], axis=0).astype(BF16)
    patch = jnp.dot(normed, hw[...], preferred_element_type=F32)
    cells = patch.shape[1]
    past = latc_ref.shape[0]
    tmp[...] = jnp.zeros_like(tmp)
    tmp[0:past, 0:cells] = latc_ref[...]
    tmp[past : past + z.frames, 0:cells] = patch[0 : z.frames]
    msg[...] = tmp[...].astype(BF16)

    order = [(dr, dc) for dr in (-1, 0, 1) for dc in (-1, 0, 1) if (dr, dc) != (0, 0)]

    def halo(dr, dc):
        at = (dr + 1) * 3 + dc + 1
        return remote(msg, near.at[8 - at], n_send.at[at], n_recv.at[8 - at], me + dc, my + dr)

    for dr, dc in order:

        @pl.when(inside(dr, dc))
        def _():
            halo(dr, dc).start()

    near[4] = msg[...]
    for copy in spread:
        copy.wait_send()
    for dr, dc in order:

        @pl.when(inside(dr, dc))
        def _():
            copy = halo(dr, dc)
            copy.wait_send()
            pltpu.make_async_remote_copy(
                src_ref=msg, dst_ref=near.at[(dr + 1) * 3 + dc + 1],
                send_sem=n_send.at[(dr + 1) * 3 + dc + 1], recv_sem=n_recv.at[(dr + 1) * 3 + dc + 1],
                device_id=(me + dc, my + dr), device_id_type=MESH,
            ).wait_recv()

    around = [near[i].astype(F32)[0:8] for i in range(9)]
    chan = cells // 4
    taps = 9 * chan
    wide_taps, rest_taps = [], []
    for i in range(2):
        for j in range(2):
            parts = [jnp.zeros((8, LANES), F32), jnp.zeros((8, LANES), F32)]
            for v in range(3):
                for u in range(3):
                    ri, ci = i + v - 1, j + u - 1
                    at = (ri // 2 + 1) * 3 + ci // 2 + 1
                    src = ((ri % 2) * 2 + ci % 2) * chan
                    to = (v * 3 + u) * chan
                    shift = (to - src) % LANES
                    cell = pltpu.roll(around[at], shift, 1) if shift else around[at]
                    inner_at = to % LANES
                    parts[to // LANES] = jnp.where(
                        (lane8 >= inner_at) & (lane8 < inner_at + chan), cell, parts[to // LANES]
                    )
            wide_taps.append(parts[0])
            rest_taps.append(parts[1])
    wide_taps = jnp.concatenate(wide_taps, axis=0).astype(BF16)
    rest_taps = jnp.concatenate(rest_taps, axis=0).astype(BF16)[:, : taps - LANES]
    steps = []
    for u in range(3):
        steps.append(
            jnp.dot(wide_taps, cw[pl.ds(u * taps, LANES), :], preferred_element_type=F32)
            + jnp.dot(rest_taps, cw[pl.ds(u * taps + LANES, taps - LANES), :], preferred_element_type=F32)
        )
    for cell in range(4):
        rows = slice(cell * 8, cell * 8 + 8)
        conv = steps[0][rows] + pltpu.roll(steps[1][rows], 7, 0) + pltpu.roll(steps[2][rows], 6, 0)
        square = jnp.sum(conv * conv, axis=1, keepdims=True) / conv.shape[1]
        scaled = conv * lax.rsqrt(square + 1e-6) * gain_ref[...]
        dec_ref[cell] = scaled / (1.0 + jnp.exp(-scaled))


def local(
    mesh, stream, queries, span_k, span_v, cache_k, cache_v, cache_age, history, out_weight,
    attn_gate, head_shift, head_scale, head_weight, latent_cache, conv_weight, rms_gain,
):
    z = Sizes(mesh, queries, cache_k, out_weight)
    span_valid = np.zeros((z.span,), np.float32)
    for slot, _, _ in z.slots():
        span_valid[slot] = 1.0
    valid = jnp.concatenate([jnp.where(cache_age < history[0], 1.0, 0.0).astype(F32), jnp.asarray(span_valid)])
    valid = jnp.tile(valid, z.halves)[None, :]
    model, chan = z.model, conv_weight.shape[1]
    past = latent_cache.shape[0]
    latc = latent_cache.reshape(past, -1).astype(F32)
    vmem = pl.BlockSpec(memory_space=pltpu.VMEM)
    hbm = pl.BlockSpec(memory_space=pl.ANY)
    half = z.all // 2
    dma = lambda *shape: pltpu.SemaphoreType.DMA(shape)
    out, dec = pl.pallas_call(
        functools.partial(kernel, z),
        out_shape=(jax.ShapeDtypeStruct((8, model), F32), jax.ShapeDtypeStruct((4, 8, chan), F32)),
        in_specs=[vmem] * 10 + [hbm] * 5,
        out_specs=(vmem, vmem),
        scratch_shapes=[
            pltpu.VMEM((z.all, z.lanes), BF16),
            pltpu.VMEM((z.all, z.lanes), BF16),
            pltpu.VMEM((z.all, z.lanes), BF16),
            pltpu.VMEM((z.all, LANES), F32),
            pltpu.VMEM((half, z.lanes), BF16),
            pltpu.VMEM((half, LANES), F32),
            pltpu.VMEM((half, z.lanes), BF16),
            pltpu.VMEM((half, LANES), F32),
            pltpu.VMEM((half, z.lanes), BF16),
            pltpu.VMEM((half, LANES), F32),
            pltpu.VMEM((z.halves * z.keys, z.lanes), BF16),
            pltpu.VMEM((z.halves * z.keys, z.lanes), BF16),
            pltpu.VMEM(out_weight.shape, BF16),
            pltpu.VMEM(head_weight.shape, BF16),
            pltpu.VMEM(conv_weight.shape, BF16),
            pltpu.VMEM((z.nhd, z.nsp * z.message, LANES), BF16),
            pltpu.VMEM((z.nhd, z.nsp * z.message, LANES), BF16),
            pltpu.VMEM((z.nsp * z.message, LANES), BF16),
            pltpu.VMEM((z.nsp * z.message, LANES), BF16),
            pltpu.VMEM((9, 16, LANES), BF16),
            pltpu.VMEM((16, LANES), BF16),
            pltpu.VMEM((16, LANES), F32),
            dma(2 * z.halves + 3),
            dma(2, z.nchip), dma(2, z.nchip), dma(2, z.nchip), dma(2, z.nchip),
            dma(2), dma(2),
            dma(2, z.nchip), dma(2, z.nchip),
            dma(z.nhd), dma(z.nhd),
            dma(z.nsp), dma(z.nsp),
            dma(9), dma(9),
        ],
        compiler_params=pltpu.CompilerParams(
            collective_id=0, has_side_effects=True, vmem_limit_bytes=56 * 1024 * 1024
        ),
        name="span_block",
    )(
        queries, span_k, span_v, valid, stream.reshape(z.frames, 1, model),
        attn_gate[None], head_shift[None], head_scale[None], latc, rms_gain[None],
        cache_k, cache_v, out_weight, head_weight, conv_weight,
    )
    stream_out = out[: z.frames].astype(BF16).reshape(stream.shape)
    decoded = jnp.transpose(dec.reshape(2, 2, 8, chan)[:, :, : z.frames], (2, 0, 1, 3)).astype(BF16)
    return stream_out, decoded


def solution(mesh):
    placed = (
        P(None, "hd", "sp", None),
        P(None, None, "sp", "hd"),
        P(None, None, "sp", "hd"),
        P(None, None, "sp", "hd"),
        P("sp", "hd"),
        P("sp", "hd"),
        P("sp"),
        P(),
        P("hd", "sp"),
        P(),
        P(),
        P(),
        P(),
        P(None, "hd", "sp", None),
        P(),
        P(),
    )
    return jax.shard_map(
        functools.partial(local, mesh),
        mesh=mesh,
        in_specs=placed,
        out_specs=(P(None, "hd", "sp", None), P(None, "hd", "sp", None)),
        check_vma=False,
    )
```

```python
import functools
import math

import jax
import jax.numpy as jnp
from jax import lax
from jax.experimental import pallas as pl
from jax.experimental.pallas import tpu as pltpu
from jax.sharding import PartitionSpec as P

HDIM = 128
LANES = 128
MESH = pl.DeviceIdType.MESH
F32 = jnp.float32
BF16 = jnp.bfloat16


def up(value, unit):
    return -(-value // unit) * unit


class Sizes:
    def __init__(self, mesh, queries, cache_k, out_weight):
        self.nsp, self.nhd = mesh.shape["sp"], mesh.shape["hd"]
        self.nchip = self.nsp // 2
        self.frames, self.rows, self.width = queries.shape
        self.heads = self.width // HDIM
        self.own = self.rows // self.nhd
        self.tokens = self.frames * self.rows
        self.slot = up(self.own * self.frames, 4)
        self.tp = self.slot * self.nhd
        self.halves = 2 if self.tp % 16 and self.heads % 2 == 0 else 1
        if self.halves == 1:
            self.tp = up(self.tp, 16)
        self.block = self.halves * self.tp
        self.lanes = self.width // self.halves
        self.pairs = self.heads // self.halves
        self.cache = cache_k.shape[0]
        self.keys = up(self.cache + up(self.tp, 16), LANES)
        self.span = self.keys - self.cache
        self.all = self.nsp * self.block
        self.part = out_weight.shape[0]
        self.pieces = -(-self.part // LANES)
        self.message = up(self.pieces * self.slot, 16)
        self.model = self.part * self.nsp

    def slots(self):
        for f in range(self.frames):
            for r in range(self.rows):
                yield (r // self.own) * self.slot + (r % self.own) * self.frames + f, f, r


def iota(shape, dim):
    return lax.broadcasted_iota(jnp.int32, shape, dim)


def merge_stats(stats):
    top = functools.reduce(jnp.maximum, stats)
    scales = [jnp.exp(s - top) for s in stats]
    total = functools.reduce(
        jnp.add, [s * pltpu.roll(a, 64, 1) for s, a in zip(stats, scales)]
    )
    return top, total, scales


def kernel(
    z, q_ref, k_ref, v_ref, age_ref, history_ref, stream_ref, gate_ref, shift_ref, scale_ref, latc_ref, gain_ref,
    ck_hbm, cv_hbm, w_hbm, hw_hbm, cw_hbm,
    so_ref, dec_ref,
    g, att, o, st, o_in, s_in, co, cs, o_got, s_got, k2, v2, w, hw, cw, zs, z_got, h, r_got, near, msg, tmp, pick_out, pick_in,
    local_sem, ag_send, ag_recv, fw_send, fw_recv, sib_send, sib_recv, b_send, b_recv,
    hd_send, hd_recv, e_send, e_recv, n_send, n_recv,
):
    me, my = lax.axis_index("sp"), lax.axis_index("hd")
    core, chip = me % 2, me // 2
    sib = me + 1 - 2 * core
    nchip, block = z.nchip, z.block

    def peer(k):
        return (chip + k) % nchip

    def source(k):
        return (chip + nchip - k) % nchip

    def rows_of(which_core, which_chip):
        return pl.ds(pl.multiple_of((which_core * nchip + which_chip) * block, block), block)

    def chip_rows(which_chip):
        return pl.ds(pl.multiple_of(which_chip * block, block), block)

    def remote(src, dst, ssem, rsem, sp, hd):
        return pltpu.make_async_remote_copy(
            src_ref=src, dst_ref=dst, send_sem=ssem, recv_sem=rsem,
            device_id=(sp, hd), device_id_type=MESH,
        )

    def packed(ref):
        row = iota((z.tp, z.width), 0)
        out = jnp.zeros((z.tp, z.width), F32)
        for slot, f, r in z.slots():
            out = jnp.where(row == slot, ref[f, r : r + 1, :].astype(F32), out)
        return [out[:, i * z.lanes : (i + 1) * z.lanes] for i in range(z.halves)]

    near[...] = jnp.zeros_like(near)

    barrier = pltpu.get_barrier_semaphore()
    for k in range(1, z.nsp):
        pl.semaphore_signal(barrier, inc=1, device_id=((me + k) % z.nsp, my), device_id_type=MESH)
    for k in range(1, z.nhd):
        pl.semaphore_signal(barrier, inc=1, device_id=(me, (my + k) % z.nhd), device_id_type=MESH)

    def inside(dr, dc):
        ok = None
        for step, at, count in ((dr, my, z.nhd), (dc, me, z.nsp)):
            if step:
                here = (at + step >= 0) & (at + step < count)
                ok = here if ok is None else ok & here
        return ok

    greeted = z.nsp - 1 + z.nhd - 1
    for dr in (-1, 1):
        for dc in (-1, 1):

            @pl.when(inside(dr, dc))
            def _():
                pl.semaphore_signal(barrier, inc=1, device_id=(me + dc, my + dr), device_id_type=MESH)

            greeted = greeted + inside(dr, dc).astype(jnp.int32)
    loads = []

    def load(src, dst):
        copy = pltpu.make_async_copy(src, dst, local_sem.at[len(loads)])
        copy.start()
        loads.append(copy)

    for half in range(z.halves):
        cols = pl.ds(half * z.lanes, z.lanes)
        load(ck_hbm.at[:, cols], k2.at[pl.ds(half * z.keys, z.cache)])
        load(cv_hbm.at[:, cols], v2.at[pl.ds(half * z.keys, z.cache)])
    attention_loads = len(loads)
    load(w_hbm, w)
    load(hw_hbm, hw)
    load(cw_hbm, cw)

    g[rows_of(core, chip), :] = jnp.concatenate(packed(q_ref), axis=0).astype(BF16)
    pl.semaphore_wait(barrier, greeted)

    def gather_start(buf, phase):
        mine = rows_of(core, chip)
        first = [
            remote(buf.at[mine], buf.at[mine], ag_send.at[phase, k], ag_recv.at[phase, k],
                   peer(k) * 2 + core, my)
            for k in range(1, nchip)
        ]
        for copy in first:
            copy.start()
        return first

    def gather_finish(buf, phase, first):
        forwards = []
        for k in range(nchip):
            if k:
                first[k - 1].wait_recv()
            rows = rows_of(core, source(k))
            copy = remote(buf.at[rows], buf.at[rows], fw_send.at[phase, k], fw_recv.at[phase, k], sib, my)
            copy.start()
            forwards.append(copy)
        for copy in forwards:
            copy.wait_recv()
        return first + forwards

    first = gather_start(g, 0)
    for ref, buf in ((k_ref, k2), (v_ref, v2)):
        for half, part in enumerate(packed(ref)):
            if z.span > z.tp:
                part = jnp.concatenate([part, jnp.zeros((z.span - z.tp, z.lanes), F32)], axis=0)
            buf[pl.ds(half * z.keys + z.cache, z.span), :] = part.astype(BF16)
    out_rows, in_rows = z.nsp * z.message, z.nsp * z.tp
    out_at, in_at = iota((out_rows, in_rows), 0), iota((out_rows, in_rows), 1)
    out_sp, inner = out_at // z.message, out_at % z.message
    wanted = in_at == ((out_sp % 2) * nchip + out_sp // 2) * z.tp + inner % z.slot
    for piece in range(z.pieces):
        picked = jnp.where(wanted & (inner // z.slot == piece), 1.0, 0.0).astype(BF16)
        pick_out[:, pl.ds(piece * in_rows, in_rows)] = picked
    to_rows, from_rows = z.nsp * 8, z.nsp * z.message
    to_at, from_at = iota((to_rows, from_rows), 0), iota((to_rows, from_rows), 1)
    wanted = from_at - (to_at // 8) * z.message - to_at % 8
    for piece in range(z.pieces):
        picked = (wanted == piece * z.slot) & (to_at % 8 < z.slot)
        pick_in[pl.ds(piece * to_rows, to_rows), :] = jnp.where(picked, 1.0, 0.0).astype(BF16)

    chunk = min(z.all, 256)
    total_keys = z.halves * z.keys
    lane = iota((chunk, LANES), 1)
    scale = 1.0 / math.sqrt(HDIM)
    key = iota((1, z.keys), 1)
    live = jnp.where(age_ref[...][None, :] < history_ref[0], 1.0, 0.0).astype(F32)
    live = jnp.concatenate([live, jnp.zeros((1, z.span), F32)], axis=1)
    for slot, _, _ in z.slots():
        live = jnp.where(key == z.cache + slot, 1.0, live)
    bounds = [jnp.broadcast_to(live, (chunk, z.keys))] * z.halves
    if z.halves > 1:
        row_half = (iota((chunk, z.keys), 0) // z.tp) % z.halves
        bounds = [jnp.where(row_half == half, b, 0.0) for half, b in enumerate(bounds)]
    mask = jnp.concatenate(bounds, axis=1) > 0.0
    ones = jnp.ones((total_keys, LANES), BF16)

    for copy in loads[:attention_loads]:
        copy.wait()
    sent = gather_finish(g, 0, first)

    def attend(at, carry):
        rows = pl.ds(pl.multiple_of(at * chunk, chunk), chunk)
        stats = jnp.zeros((chunk, LANES), F32)
        for j in range(z.pairs):
            cols = pl.ds(j * HDIM, HDIM)
            scores = lax.dot_general(
                g[rows, cols], k2[:, cols], (((1,), (1,)), ((), ())), preferred_element_type=F32
            )
            scores = jnp.where(mask, scores * scale, -1e30)
            top = jnp.max(scores, axis=1, keepdims=True)
            weights = jnp.exp(scores - top).astype(BF16)
            out = jnp.dot(
                weights, jnp.concatenate([v2[:, cols], ones], axis=1), preferred_element_type=F32
            )
            total = out[:, HDIM:]
            o[rows, cols] = out[:, :HDIM].astype(BF16)
            stats = jnp.where(lane == j, top, jnp.where(lane == j + 64, total, stats))
        st[rows, :] = stats
        return carry

    lax.fori_loop(0, z.all // chunk, attend, 0)

    half_rows = nchip * block
    theirs = pl.ds(pl.multiple_of((1 - core) * half_rows, half_rows), half_rows)
    pair = [
        remote(st.at[theirs], s_in, sib_send.at[0], sib_recv.at[0], sib, my),
        remote(o.at[theirs], o_in, sib_send.at[1], sib_recv.at[1], sib, my),
    ]
    for copy in pair:
        copy.start()
    for copy in sent:
        copy.wait_send()
    for copy in pair:
        copy.wait_recv()

    low = iota((block, LANES), 1) < 64
    exchanged = []
    for k in list(range(1, nchip)) + [0]:
        to = peer(k)
        mine, rows = rows_of(core, to), chip_rows(to)
        top, total, (a, b) = merge_stats([st[mine, :], s_in[rows, :]])
        cs[rows, :] = jnp.where(low, top, total)
        for j in range(z.pairs):
            cols = pl.ds(j * HDIM, HDIM)
            merged = (
                o[mine, cols].astype(F32) * a[:, j : j + 1]
                + o_in[rows, cols].astype(F32) * b[:, j : j + 1]
            )
            co[rows, cols] = merged.astype(BF16)
        if k:
            there = chip_rows(chip)
            for which, (src, dst) in enumerate(((cs, s_got), (co, o_got))):
                copy = remote(src.at[rows], dst.at[there], b_send.at[which, k], b_recv.at[which, k],
                              to * 2 + core, my)
                copy.start()
                exchanged.append(copy)
    own_rows = chip_rows(chip)
    s_got[own_rows, :] = cs[own_rows, :]
    o_got[own_rows, :] = co[own_rows, :]
    for copy in exchanged:
        copy.wait_recv()

    top, total, scales = merge_stats([s_got[pl.ds(i * block, block), :] for i in range(nchip)])
    inverse = pltpu.roll(1.0 / jnp.where(low, 1.0, total), 64, 1)
    for j in range(z.pairs):
        cols = pl.ds(j * HDIM, HDIM)
        summed = functools.reduce(
            jnp.add,
            [
                o_got[pl.ds(i * block, block), cols].astype(F32) * scales[i][:, j : j + 1]
                for i in range(nchip)
            ],
        )
        att[rows_of(core, chip), cols] = (summed * inverse[:, j : j + 1]).astype(BF16)

    first = gather_start(att, 1)
    for copy in pair + exchanged:
        copy.wait_send()
    for copy in loads[attention_loads:]:
        copy.wait()
    sent = gather_finish(att, 1, first)

    everything = att[...]
    proj = None
    for half in range(z.halves):
        term = lax.dot_general(
            everything, w[:, pl.ds(half * z.lanes, z.lanes)], (((1,), (1,)), ((), ())),
            preferred_element_type=F32,
        )
        term = term.reshape(z.nsp, z.halves, z.tp, z.part)[:, half]
        proj = term if proj is None else proj + term
    proj = proj.reshape(z.nsp * z.tp, z.part)
    wide = z.pieces * LANES
    if wide > z.part:
        proj = jnp.concatenate([proj, jnp.zeros((in_rows, wide - z.part), F32)], axis=1)
    owned = []
    for owner in range(z.nhd):
        turned = pltpu.roll(proj, in_rows - owner * z.slot, 0) if owner else proj
        turned = turned.astype(BF16)
        owned.append(
            jnp.concatenate([turned[:, i * LANES : (i + 1) * LANES] for i in range(z.pieces)], axis=0)
        )
    moved = jnp.dot(pick_out[...], jnp.concatenate(owned, axis=1), preferred_element_type=F32).astype(BF16)
    for owner in range(z.nhd):
        zs[owner] = moved[:, owner * LANES : (owner + 1) * LANES]

    swaps = []
    for k in range(1, z.nhd):
        to = (my + k) % z.nhd
        copy = remote(zs.at[to], z_got.at[my], hd_send.at[k], hd_recv.at[k], me, to)
        copy.start()
        swaps.append(copy)
    for copy in sent:
        copy.wait_send()
    summed = zs[my].astype(F32)
    for k in range(1, z.nhd):
        swaps[k - 1].wait_recv()
        summed = summed + z_got[(my + z.nhd - k) % z.nhd].astype(F32)
    h[...] = summed.astype(BF16)

    def message_rows(at):
        return pl.ds(pl.multiple_of(at * z.message, z.message), z.message)

    spread = []
    for k in range(1, z.nsp):
        to = (me + k) % z.nsp
        copy = remote(h.at[message_rows(to)], r_got.at[message_rows(me)], e_send.at[k], e_recv.at[k], to, my)
        copy.start()
        spread.append(copy)
    r_got[message_rows(me), :] = h[message_rows(me), :]
    for copy in swaps:
        copy.wait_send()
    for copy in spread:
        copy.wait_recv()

    picked = jnp.dot(pick_in[...], r_got[...], preferred_element_type=F32)
    by_piece = [picked[i * to_rows : (i + 1) * to_rows] for i in range(z.pieces)]
    lane8 = iota((8, LANES), 1)
    row8 = iota((8, LANES), 0)
    tiles = []
    for tile in range(z.model // LANES):
        value = jnp.zeros((8, LANES), F32)
        begin = tile * LANES
        for s in range(begin // z.part, (begin + LANES - 1) // z.part + 1):
            for piece in range(z.pieces):
                low_at = s * z.part + piece * LANES
                high_at = min(low_at + LANES, (s + 1) * z.part)
                a, b = max(low_at, begin), min(high_at, begin + LANES)
                if a >= b:
                    continue
                cell = by_piece[piece][s * 8 : (s + 1) * 8]
                if (low_at - begin) % LANES:
                    cell = pltpu.roll(cell, (low_at - begin) % LANES, 1)
                value = jnp.where((lane8 >= a - begin) & (lane8 < b - begin), cell, value)
        cols = pl.ds(begin, LANES)
        base_value = jnp.zeros((8, LANES), F32)
        for f in range(z.frames):
            base_value = jnp.where(row8 == f, stream_ref[f : f + 1, cols].astype(F32), base_value)
        value = base_value + gate_ref[:, cols] * value
        rounded = value.astype(BF16)
        so_ref[:, cols] = rounded[: z.frames]
        value = rounded.astype(F32)
        tiles.append(value)
    mean = jnp.sum(functools.reduce(jnp.add, tiles), axis=1, keepdims=True) / z.model
    centred = [t - mean for t in tiles]
    variance = jnp.sum(functools.reduce(jnp.add, [t * t for t in centred]), axis=1, keepdims=True) / z.model
    root = lax.rsqrt(variance + 1e-6)
    normed = []
    for tile, t in enumerate(centred):
        cols = pl.ds(tile * LANES, LANES)
        normed.append(t * root * (1.0 + scale_ref[:, cols]) + shift_ref[:, cols])
    normed = jnp.concatenate(normed, axis=1)
    normed = jnp.concatenate([normed, jnp.zeros_like(normed)], axis=0).astype(BF16)
    patch = lax.dot_general(
        normed, hw[...], (((1,), (1,)), ((), ())), preferred_element_type=F32
    )
    cells = patch.shape[1]
    past = latc_ref.shape[0]
    tmp[...] = jnp.zeros_like(tmp)
    chan = cells // 4
    for f in range(past):
        for a in range(2):
            for b in range(2):
                at = (a * 2 + b) * chan
                tmp[f : f + 1, at : at + chan] = latc_ref[f, a, b : b + 1, :].astype(F32)
    tmp[past : past + z.frames, 0:cells] = patch[0 : z.frames]
    msg[...] = tmp[...].astype(BF16)

    order = [(dr, dc) for dr in (-1, 0, 1) for dc in (-1, 0, 1) if (dr, dc) != (0, 0)]

    def halo(dr, dc):
        at = (dr + 1) * 3 + dc + 1
        return remote(msg, near.at[8 - at], n_send.at[at], n_recv.at[8 - at], me + dc, my + dr)

    for dr, dc in order:

        @pl.when(inside(dr, dc))
        def _():
            halo(dr, dc).start()

    near[4] = msg[...]
    for copy in spread:
        copy.wait_send()
    for dr, dc in order:

        @pl.when(inside(dr, dc))
        def _():
            copy = halo(dr, dc)
            copy.wait_send()
            pltpu.make_async_remote_copy(
                src_ref=msg, dst_ref=near.at[(dr + 1) * 3 + dc + 1],
                send_sem=n_send.at[(dr + 1) * 3 + dc + 1], recv_sem=n_recv.at[(dr + 1) * 3 + dc + 1],
                device_id=(me + dc, my + dr), device_id_type=MESH,
            ).wait_recv()

    around = [near[i].astype(F32)[0:8] for i in range(9)]
    taps = 9 * chan
    wide_taps, rest_taps = [], []
    for i in range(2):
        for j in range(2):
            parts = [jnp.zeros((8, LANES), F32), jnp.zeros((8, LANES), F32)]
            for v in range(3):
                for u in range(3):
                    ri, ci = i + v - 1, j + u - 1
                    at = (ri // 2 + 1) * 3 + ci // 2 + 1
                    src = ((ri % 2) * 2 + ci % 2) * chan
                    to = (v * 3 + u) * chan
                    shift = (to - src) % LANES
                    cell = pltpu.roll(around[at], shift, 1) if shift else around[at]
                    inner_at = to % LANES
                    parts[to // LANES] = jnp.where(
                        (lane8 >= inner_at) & (lane8 < inner_at + chan), cell, parts[to // LANES]
                    )
            wide_taps.append(parts[0])
            rest_taps.append(parts[1])
    wide_taps = jnp.concatenate(wide_taps, axis=0).astype(BF16)
    rest_taps = jnp.concatenate(rest_taps, axis=0).astype(BF16)[:, : taps - LANES]
    steps = []
    for u in range(3):
        steps.append(
            jnp.dot(wide_taps, cw[pl.ds(u * taps, LANES), :], preferred_element_type=F32)
            + jnp.dot(rest_taps, cw[pl.ds(u * taps + LANES, taps - LANES), :], preferred_element_type=F32)
        )
    gain = gain_ref[...][None, :]
    decoded = []
    for cell in range(4):
        rows = slice(cell * 8, cell * 8 + 8)
        conv = steps[0][rows] + pltpu.roll(steps[1][rows], 7, 0) + pltpu.roll(steps[2][rows], 6, 0)
        square = jnp.sum(conv * conv, axis=1, keepdims=True) / conv.shape[1]
        scaled = conv * lax.rsqrt(square + 1e-6) * gain
        decoded.append(scaled / (1.0 + jnp.exp(-scaled)))
    for f in range(z.frames):
        for i in range(2):
            pair_of = [decoded[i * 2 + j][f : f + 1] for j in range(2)]
            dec_ref[f, i] = jnp.concatenate(pair_of, axis=0).astype(BF16)


def local(
    mesh, stream, queries, span_k, span_v, cache_k, cache_v, cache_age, history, out_weight,
    attn_gate, head_shift, head_scale, head_weight, latent_cache, conv_weight, rms_gain,
):
    queries, span_k, span_v = (t[:, :, 0] for t in (queries, span_k, span_v))
    out_weight, head_weight = out_weight.T, head_weight.T
    z = Sizes(mesh, queries, cache_k, out_weight)
    model, chan = z.model, conv_weight.shape[1]
    vmem = pl.BlockSpec(memory_space=pltpu.VMEM)
    hbm = pl.BlockSpec(memory_space=pl.ANY)
    half = z.all // 2
    dma = lambda *shape: pltpu.SemaphoreType.DMA(shape)
    out, dec = pl.pallas_call(
        functools.partial(kernel, z),
        out_shape=(
            jax.ShapeDtypeStruct((z.frames, model), BF16),
            jax.ShapeDtypeStruct((z.frames, 2, 2, chan), BF16),
        ),
        in_specs=[vmem] * 4 + [pl.BlockSpec(memory_space=pltpu.SMEM)] + [vmem] * 6 + [hbm] * 5,
        out_specs=(vmem, vmem),
        scratch_shapes=[
            pltpu.VMEM((z.all, z.lanes), BF16),
            pltpu.VMEM((z.all, z.lanes), BF16),
            pltpu.VMEM((z.all, z.lanes), BF16),
            pltpu.VMEM((z.all, LANES), F32),
            pltpu.VMEM((half, z.lanes), BF16),
            pltpu.VMEM((half, LANES), F32),
            pltpu.VMEM((half, z.lanes), BF16),
            pltpu.VMEM((half, LANES), F32),
            pltpu.VMEM((half, z.lanes), BF16),
            pltpu.VMEM((half, LANES), F32),
            pltpu.VMEM((z.halves * z.keys, z.lanes), BF16),
            pltpu.VMEM((z.halves * z.keys, z.lanes), BF16),
            pltpu.VMEM(out_weight.shape, BF16),
            pltpu.VMEM(head_weight.shape, BF16),
            pltpu.VMEM(conv_weight.shape, BF16),
            pltpu.VMEM((z.nhd, z.nsp * z.message, LANES), BF16),
            pltpu.VMEM((z.nhd, z.nsp * z.message, LANES), BF16),
            pltpu.VMEM((z.nsp * z.message, LANES), BF16),
            pltpu.VMEM((z.nsp * z.message, LANES), BF16),
            pltpu.VMEM((9, 16, LANES), BF16),
            pltpu.VMEM((16, LANES), BF16),
            pltpu.VMEM((16, LANES), F32),
            pltpu.VMEM((z.nsp * z.message, z.pieces * z.nsp * z.tp), BF16),
            pltpu.VMEM((z.pieces * z.nsp * 8, z.nsp * z.message), BF16),
            dma(2 * z.halves + 3),
            dma(2, z.nchip), dma(2, z.nchip), dma(2, z.nchip), dma(2, z.nchip),
            dma(2), dma(2),
            dma(2, z.nchip), dma(2, z.nchip),
            dma(z.nhd), dma(z.nhd),
            dma(z.nsp), dma(z.nsp),
            dma(9), dma(9),
        ],
        compiler_params=pltpu.CompilerParams(
            collective_id=0, has_side_effects=True, vmem_limit_bytes=56 * 1024 * 1024
        ),
        name="span_block",
    )(
        queries, span_k, span_v, cache_age, history, stream.reshape(z.frames, model),
        attn_gate[None], head_shift[None], head_scale[None], latent_cache, rms_gain,
        cache_k, cache_v, out_weight, head_weight, conv_weight,
    )
    return out.reshape(stream.shape), dec


def solution(mesh):
    placed = (
        P(None, "hd", "sp", None),
        P(None, None, "sp", "hd"),
        P(None, None, "sp", "hd"),
        P(None, None, "sp", "hd"),
        P("sp", "hd"),
        P("sp", "hd"),
        P("sp"),
        P(),
        P("hd", "sp"),
        P(),
        P(),
        P(),
        P(),
        P(None, "hd", "sp", None),
        P(),
        P(),
    )
    return jax.shard_map(
        functools.partial(local, mesh),
        mesh=mesh,
        in_specs=placed,
        out_specs=(P(None, "hd", "sp", None), P(None, "hd", "sp", None)),
        check_vma=False,
    )
```

```python
import functools
import math

import jax
import jax.numpy as jnp
from jax import lax
from jax.experimental import pallas as pl
from jax.experimental.pallas import tpu as pltpu
from jax.sharding import PartitionSpec as P

HDIM = 128
LANES = 128
MESH = pl.DeviceIdType.MESH
F32 = jnp.float32
BF16 = jnp.bfloat16


def up(value, unit):
    return -(-value // unit) * unit


class Sizes:
    def __init__(self, mesh, queries, cache_k, out_weight):
        self.nsp, self.nhd = mesh.shape["sp"], mesh.shape["hd"]
        self.nchip = self.nsp // 2
        self.frames, self.rows, self.width = queries.shape
        self.heads = self.width // HDIM
        self.own = self.rows // self.nhd
        self.tokens = self.frames * self.rows
        self.slot = up(self.own * self.frames, 4)
        self.tp = self.slot * self.nhd
        self.halves = 2 if self.tp % 16 and self.heads % 2 == 0 else 1
        if self.halves == 1:
            self.tp = up(self.tp, 16)
        self.block = self.halves * self.tp
        self.lanes = self.width // self.halves
        self.pairs = self.heads // self.halves
        self.chunks = 1 if self.pairs % 2 else 2
        self.chunk_pairs = self.pairs // self.chunks
        self.wide = self.lanes // self.chunks
        self.cache = cache_k.shape[0]
        self.keys = up(self.cache + up(self.tp, 16), LANES)
        self.span = self.keys - self.cache
        self.all = self.nsp * self.block
        self.part = out_weight.shape[0]
        self.pieces = -(-self.part // LANES)
        self.message = up(self.pieces * self.slot, 16)
        self.model = self.part * self.nsp

    def slots(self):
        for f in range(self.frames):
            for r in range(self.rows):
                yield (r // self.own) * self.slot + (r % self.own) * self.frames + f, f, r


def iota(shape, dim):
    return lax.broadcasted_iota(jnp.int32, shape, dim)


def merge_stats(stats):
    top = functools.reduce(jnp.maximum, stats)
    scales = [jnp.exp(s - top) for s in stats]
    total = functools.reduce(
        jnp.add, [s * pltpu.roll(a, 64, 1) for s, a in zip(stats, scales)]
    )
    return top, total, scales


def kernel(
    z, q_ref, k_ref, v_ref, age_ref, history_ref, stream_ref, gate_ref, shift_ref, scale_ref, latc_ref, gain_ref,
    ck_hbm, cv_hbm, w_hbm, hw_hbm, cw_hbm,
    so_ref, dec_ref,
    g, att, o, o_in, co, o_got, k2, v2, w, hw, cw, zs, z_got, h, r_got, near, msg, tmp, pick_out, pick_in,
    local_sem, z_send, z_recv, x_send, x_recv, c_send, c_recv, sib_send, sib_recv, b_send, b_recv,
    hd_send, hd_recv, e_send, e_recv, n_send, n_recv,
):
    me, my = lax.axis_index("sp"), lax.axis_index("hd")
    core, chip = me % 2, me // 2
    sib = me + 1 - 2 * core
    nchip, block = z.nchip, z.block

    def peer(k):
        return (chip + k) % nchip

    def source(k):
        return (chip + nchip - k) % nchip

    def rows_of(which_core, which_chip):
        return pl.ds(pl.multiple_of((which_core * nchip + which_chip) * block, block), block)

    def chip_rows(which_chip):
        return pl.ds(pl.multiple_of(which_chip * block, block), block)

    def remote(src, dst, ssem, rsem, sp, hd):
        return pltpu.make_async_remote_copy(
            src_ref=src, dst_ref=dst, send_sem=ssem, recv_sem=rsem,
            device_id=(sp, hd), device_id_type=MESH,
        )

    def packed(ref):
        row = iota((z.tp, z.width), 0)
        out = jnp.zeros((z.tp, z.width), F32)
        for slot, f, r in z.slots():
            out = jnp.where(row == slot, ref[f, r : r + 1, :].astype(F32), out)
        return [out[:, i * z.lanes : (i + 1) * z.lanes] for i in range(z.halves)]

    near[...] = jnp.zeros_like(near)

    barrier = pltpu.get_barrier_semaphore()
    for k in range(1, z.nsp):
        pl.semaphore_signal(barrier, inc=1, device_id=((me + k) % z.nsp, my), device_id_type=MESH)
    for k in range(1, z.nhd):
        pl.semaphore_signal(barrier, inc=1, device_id=(me, (my + k) % z.nhd), device_id_type=MESH)

    def inside(dr, dc):
        ok = None
        for step, at, count in ((dr, my, z.nhd), (dc, me, z.nsp)):
            if step:
                here = (at + step >= 0) & (at + step < count)
                ok = here if ok is None else ok & here
        return ok

    greeted = z.nsp - 1 + z.nhd - 1
    for dr in (-1, 1):
        for dc in (-1, 1):

            @pl.when(inside(dr, dc))
            def _():
                pl.semaphore_signal(barrier, inc=1, device_id=(me + dc, my + dr), device_id_type=MESH)

            greeted = greeted + inside(dr, dc).astype(jnp.int32)
    loads = []

    def load(src, dst):
        copy = pltpu.make_async_copy(src, dst, local_sem.at[len(loads)])
        copy.start()
        loads.append(copy)

    for half in range(z.halves):
        cols = pl.ds(half * z.lanes, z.lanes)
        load(ck_hbm.at[:, cols], k2.at[pl.ds(half * z.keys, z.cache)])
        load(cv_hbm.at[:, cols], v2.at[pl.ds(half * z.keys, z.cache)])
    attention_loads = len(loads)
    load(w_hbm, w)
    load(hw_hbm, hw)
    load(cw_hbm, cw)

    mine_q = jnp.concatenate(packed(q_ref), axis=0).astype(BF16)
    for ch in range(z.chunks):
        g[ch, rows_of(core, chip), :] = mine_q[:, ch * z.wide : (ch + 1) * z.wide]
    pl.semaphore_wait(barrier, greeted)

    far, side = nchip // 2, chip % 2
    partner = (chip + 1 - 2 * side) * 2 + core
    pending = []

    def distant(k):
        return (chip // 2 + far - k) % far

    def pass_on(buf, phase, ch, at_core, at_chip, sems, slot, to):
        rows = rows_of(at_core, at_chip)
        ssem, rsem = sems
        copy = remote(buf.at[ch, rows], buf.at[ch, rows], ssem.at[phase, ch, slot], rsem.at[phase, ch, slot], to, my)
        copy.start()
        pending.append(copy)
        return copy

    along, across, within = (z_send, z_recv), (x_send, x_recv), (c_send, c_recv)

    class Gather:
        def __init__(self, buf, phase, ch):
            self.at = (buf, phase, ch)
            self.z = [
                pass_on(*self.at, core, chip, along, k, (((chip // 2 + k) % far) * 2 + side) * 2 + core)
                for k in range(1, far)
            ]
            self.x = [pass_on(*self.at, core, chip, across, 0, partner)]
            self.c = [pass_on(*self.at, core, chip, within, 0, sib)]

        def relay_z(self):
            for k in range(1, far):
                self.z[k - 1].wait_recv()
                from_chip = distant(k) * 2 + side
                self.x.append(pass_on(*self.at, core, from_chip, across, k, partner))
                self.c.append(pass_on(*self.at, core, from_chip, within, k, sib))

        def relay_x(self):
            for k in range(far):
                self.x[k].wait_recv()
                from_chip = distant(k) * 2 + 1 - side
                self.c.append(pass_on(*self.at, core, from_chip, within, far + k, sib))

        def finish(self):
            for copy in self.c:
                copy.wait_recv()

    asked = [Gather(g, 0, ch) for ch in range(z.chunks)]
    for ref, buf in ((k_ref, k2), (v_ref, v2)):
        for half, part in enumerate(packed(ref)):
            if z.span > z.tp:
                part = jnp.concatenate([part, jnp.zeros((z.span - z.tp, z.lanes), F32)], axis=0)
            buf[pl.ds(half * z.keys + z.cache, z.span), :] = part.astype(BF16)
    out_rows, in_rows = z.nsp * z.message, z.nsp * z.tp
    out_at, in_at = iota((out_rows, in_rows), 0), iota((out_rows, in_rows), 1)
    out_sp, inner = out_at // z.message, out_at % z.message
    wanted = in_at == ((out_sp % 2) * nchip + out_sp // 2) * z.tp + inner % z.slot
    for piece in range(z.pieces):
        picked = jnp.where(wanted & (inner // z.slot == piece), 1.0, 0.0).astype(BF16)
        pick_out[:, pl.ds(piece * in_rows, in_rows)] = picked
    to_rows, from_rows = z.nsp * 8, z.nsp * z.message
    to_at, from_at = iota((to_rows, from_rows), 0), iota((to_rows, from_rows), 1)
    wanted = from_at - (to_at // 8) * z.message - to_at % 8
    for piece in range(z.pieces):
        picked = (wanted == piece * z.slot) & (to_at % 8 < z.slot)
        pick_in[pl.ds(piece * to_rows, to_rows), :] = jnp.where(picked, 1.0, 0.0).astype(BF16)

    chunk = min(z.all, 256)
    total_keys = z.halves * z.keys
    lane = iota((chunk, LANES), 1)
    scale = 1.0 / math.sqrt(HDIM)
    key = iota((1, z.keys), 1)
    live = jnp.where(age_ref[...][None, :] < history_ref[0], 1.0, 0.0).astype(F32)
    live = jnp.concatenate([live, jnp.zeros((1, z.span), F32)], axis=1)
    for slot, _, _ in z.slots():
        live = jnp.where(key == z.cache + slot, 1.0, live)
    bounds = [jnp.broadcast_to(live, (chunk, z.keys))] * z.halves
    if z.halves > 1:
        row_half = (iota((chunk, z.keys), 0) // z.tp) % z.halves
        bounds = [jnp.where(row_half == half, b, 0.0) for half, b in enumerate(bounds)]
    mask = jnp.concatenate(bounds, axis=1) > 0.0
    ones = jnp.ones((total_keys, LANES), BF16)

    asked[0].relay_z()
    for copy in loads[:attention_loads]:
        copy.wait()
    asked[0].relay_x()
    asked[0].finish()

    def attend(ch, pairs):
        def step(at, carry):
            rows = pl.ds(pl.multiple_of(at * chunk, chunk), chunk)
            stat_cols = pl.ds(z.wide, LANES)
            stats = o[ch, rows, stat_cols].astype(F32) if pairs[0] else jnp.zeros((chunk, LANES), F32)
            for j in pairs:
                near_cols = pl.ds(j * HDIM, HDIM)
                cols = pl.ds(ch * z.wide + j * HDIM, HDIM)
                scores = lax.dot_general(
                    g[ch, rows, near_cols], k2[:, cols], (((1,), (1,)), ((), ())), preferred_element_type=F32
                )
                scores = jnp.where(mask, scores * scale, -1e30)
                top = jnp.max(scores, axis=1, keepdims=True).astype(BF16).astype(F32)
                weights = jnp.exp(scores - top).astype(BF16)
                out = jnp.dot(
                    weights, jnp.concatenate([v2[:, cols], ones], axis=1), preferred_element_type=F32
                )
                o[ch, rows, near_cols] = out[:, :HDIM].astype(BF16)
                stats = jnp.where(lane == j, top, jnp.where(lane == j + 64, out[:, HDIM:], stats))
            o[ch, rows, stat_cols] = stats.astype(BF16)
            return carry

        if z.all == chunk:
            step(0, 0)
        else:
            lax.fori_loop(0, z.all // chunk, step, 0)

    half_rows = nchip * block
    theirs = pl.ds(pl.multiple_of((1 - core) * half_rows, half_rows), half_rows)
    low = iota((block, LANES), 1) < 64

    def give(ch):
        copy = remote(o.at[ch, theirs], o_in.at[ch], sib_send.at[ch], sib_recv.at[ch], sib, my)
        copy.start()
        pending.append(copy)
        return copy

    def merge(ch, given):
        given.wait_recv()
        stat_cols = pl.ds(z.wide, LANES)
        copies = []
        for k in list(range(1, nchip)) + [0]:
            to = peer(k)
            mine, rows = rows_of(core, to), chip_rows(to)
            top, total, (a, b) = merge_stats(
                [o[ch, mine, stat_cols].astype(F32), o_in[ch, rows, stat_cols].astype(F32)]
            )
            dst, at = (co, rows) if k else (o_got, chip_rows(chip))
            dst[ch, at, stat_cols] = jnp.where(low, top, total).astype(BF16)
            for j in range(z.chunk_pairs):
                cols = pl.ds(j * HDIM, HDIM)
                merged = (
                    o[ch, mine, cols].astype(F32) * a[:, j : j + 1]
                    + o_in[ch, rows, cols].astype(F32) * b[:, j : j + 1]
                )
                dst[ch, at, cols] = merged.astype(BF16)
            if k:
                copy = remote(co.at[ch, rows], o_got.at[ch, chip_rows(chip)], b_send.at[ch, k], b_recv.at[ch, k],
                              to * 2 + core, my)
                copy.start()
                copies.append(copy)
        pending.extend(copies)
        return copies

    def settle(ch, copies):
        for copy in copies:
            copy.wait_recv()
        parts = [pl.ds(i * block, block) for i in range(nchip)]
        top, total, scales = merge_stats([o_got[ch, p, pl.ds(z.wide, LANES)].astype(F32) for p in parts])
        inverse = pltpu.roll(1.0 / jnp.where(low, 1.0, total), 64, 1)
        for j in range(z.chunk_pairs):
            cols = pl.ds(j * HDIM, HDIM)
            terms = [o_got[ch, p, cols].astype(F32) * s[:, j : j + 1] for p, s in zip(parts, scales)]
            summed = functools.reduce(jnp.add, terms)
            att[ch, rows_of(core, chip), cols] = (summed * inverse[:, j : j + 1]).astype(BF16)
        return Gather(att, 1, ch)

    cut = max(1, z.chunk_pairs // 2)
    first_pairs, last_pairs = range(cut), range(cut, z.chunk_pairs)
    given, partials, shared = [], [], []
    for ch in range(z.chunks):
        if ch:
            asked[ch].finish()
        more = ch + 1 < z.chunks
        if more:
            asked[ch + 1].relay_z()
        attend(ch, first_pairs)
        if ch:
            partials.append(merge(ch - 1, given[ch - 1]))
        if more:
            asked[ch + 1].relay_x()
        attend(ch, last_pairs)
        given.append(give(ch))
    partials.append(merge(z.chunks - 1, given[-1]))
    for ch in range(z.chunks):
        shared.append(settle(ch, partials[ch]))
        if ch:
            shared[ch - 1].relay_x()
        shared[ch].relay_z()
    shared[-1].relay_x()

    for copy in loads[attention_loads:]:
        copy.wait()
    proj = [None] * z.halves
    for ch in range(z.chunks):
        shared[ch].finish()
        for half in range(z.halves):
            term = lax.dot_general(
                att[ch], w[:, pl.ds(half * z.lanes + ch * z.wide, z.wide)], (((1,), (1,)), ((), ())),
                preferred_element_type=F32,
            )
            proj[half] = term if proj[half] is None else proj[half] + term
    picked = [p.reshape(z.nsp, z.halves, z.tp, z.part)[:, half] for half, p in enumerate(proj)]
    proj = functools.reduce(jnp.add, picked)
    proj = proj.reshape(z.nsp * z.tp, z.part)
    wide = z.pieces * LANES
    if wide > z.part:
        proj = jnp.concatenate([proj, jnp.zeros((in_rows, wide - z.part), F32)], axis=1)
    owned = []
    for owner in range(z.nhd):
        turned = pltpu.roll(proj, in_rows - owner * z.slot, 0) if owner else proj
        turned = turned.astype(BF16)
        owned.append(
            jnp.concatenate([turned[:, i * LANES : (i + 1) * LANES] for i in range(z.pieces)], axis=0)
        )
    moved = jnp.dot(pick_out[...], jnp.concatenate(owned, axis=1), preferred_element_type=F32).astype(BF16)
    for owner in range(z.nhd):
        zs[owner] = moved[:, owner * LANES : (owner + 1) * LANES]

    swaps = []
    for k in range(1, z.nhd):
        to = (my + k) % z.nhd
        copy = remote(zs.at[to], z_got.at[my], hd_send.at[k], hd_recv.at[k], me, to)
        copy.start()
        swaps.append(copy)
    summed = zs[my].astype(F32)
    for k in range(1, z.nhd):
        swaps[k - 1].wait_recv()
        summed = summed + z_got[(my + z.nhd - k) % z.nhd].astype(F32)
    h[...] = summed.astype(BF16)

    def message_rows(at):
        return pl.ds(pl.multiple_of(at * z.message, z.message), z.message)

    spread = []
    for k in range(1, z.nsp):
        to = (me + k) % z.nsp
        copy = remote(h.at[message_rows(to)], r_got.at[message_rows(me)], e_send.at[k], e_recv.at[k], to, my)
        copy.start()
        spread.append(copy)
    r_got[message_rows(me), :] = h[message_rows(me), :]
    pending.extend(swaps)
    pending.extend(spread)
    for copy in spread:
        copy.wait_recv()

    picked = jnp.dot(pick_in[...], r_got[...], preferred_element_type=F32)
    by_piece = [picked[i * to_rows : (i + 1) * to_rows] for i in range(z.pieces)]
    lane8 = iota((8, LANES), 1)
    row8 = iota((8, LANES), 0)
    tiles = []
    for tile in range(z.model // LANES):
        value = jnp.zeros((8, LANES), F32)
        begin = tile * LANES
        for s in range(begin // z.part, (begin + LANES - 1) // z.part + 1):
            for piece in range(z.pieces):
                low_at = s * z.part + piece * LANES
                high_at = min(low_at + LANES, (s + 1) * z.part)
                a, b = max(low_at, begin), min(high_at, begin + LANES)
                if a >= b:
                    continue
                cell = by_piece[piece][s * 8 : (s + 1) * 8]
                if (low_at - begin) % LANES:
                    cell = pltpu.roll(cell, (low_at - begin) % LANES, 1)
                value = jnp.where((lane8 >= a - begin) & (lane8 < b - begin), cell, value)
        cols = pl.ds(begin, LANES)
        base_value = jnp.zeros((8, LANES), F32)
        for f in range(z.frames):
            base_value = jnp.where(row8 == f, stream_ref[f : f + 1, cols].astype(F32), base_value)
        value = base_value + gate_ref[:, cols] * value
        rounded = value.astype(BF16)
        so_ref[:, cols] = rounded[: z.frames]
        value = rounded.astype(F32)
        tiles.append(value)
    mean = jnp.sum(functools.reduce(jnp.add, tiles), axis=1, keepdims=True) / z.model
    centred = [t - mean for t in tiles]
    variance = jnp.sum(functools.reduce(jnp.add, [t * t for t in centred]), axis=1, keepdims=True) / z.model
    root = lax.rsqrt(variance + 1e-6)
    normed = []
    for tile, t in enumerate(centred):
        cols = pl.ds(tile * LANES, LANES)
        normed.append(t * root * (1.0 + scale_ref[:, cols]) + shift_ref[:, cols])
    normed = jnp.concatenate(normed, axis=1)
    normed = jnp.concatenate([normed, jnp.zeros_like(normed)], axis=0).astype(BF16)
    patch = lax.dot_general(
        normed, hw[...], (((1,), (1,)), ((), ())), preferred_element_type=F32
    )
    cells = patch.shape[1]
    past = latc_ref.shape[0]
    tmp[...] = jnp.zeros_like(tmp)
    chan = cells // 4
    for f in range(past):
        for a in range(2):
            for b in range(2):
                at = (a * 2 + b) * chan
                tmp[f : f + 1, at : at + chan] = latc_ref[f, a, b : b + 1, :].astype(F32)
    tmp[past : past + z.frames, 0:cells] = patch[0 : z.frames]
    msg[...] = tmp[...].astype(BF16)

    order = [(dr, dc) for dr in (-1, 0, 1) for dc in (-1, 0, 1) if (dr, dc) != (0, 0)]

    def halo(dr, dc):
        at = (dr + 1) * 3 + dc + 1
        return remote(msg, near.at[8 - at], n_send.at[at], n_recv.at[8 - at], me + dc, my + dr)

    for dr, dc in order:

        @pl.when(inside(dr, dc))
        def _():
            halo(dr, dc).start()

    near[4] = msg[...]
    for dr, dc in order:

        @pl.when(inside(dr, dc))
        def _():
            copy = halo(dr, dc)
            copy.wait_send()
            pltpu.make_async_remote_copy(
                src_ref=msg, dst_ref=near.at[(dr + 1) * 3 + dc + 1],
                send_sem=n_send.at[(dr + 1) * 3 + dc + 1], recv_sem=n_recv.at[(dr + 1) * 3 + dc + 1],
                device_id=(me + dc, my + dr), device_id_type=MESH,
            ).wait_recv()

    around = [near[i].astype(F32)[0:8] for i in range(9)]
    taps = 9 * chan
    wide_taps, rest_taps = [], []
    for i in range(2):
        for j in range(2):
            parts = [jnp.zeros((8, LANES), F32), jnp.zeros((8, LANES), F32)]
            for v in range(3):
                for u in range(3):
                    ri, ci = i + v - 1, j + u - 1
                    at = (ri // 2 + 1) * 3 + ci // 2 + 1
                    src = ((ri % 2) * 2 + ci % 2) * chan
                    to = (v * 3 + u) * chan
                    shift = (to - src) % LANES
                    cell = pltpu.roll(around[at], shift, 1) if shift else around[at]
                    inner_at = to % LANES
                    parts[to // LANES] = jnp.where(
                        (lane8 >= inner_at) & (lane8 < inner_at + chan), cell, parts[to // LANES]
                    )
            wide_taps.append(parts[0])
            rest_taps.append(parts[1])
    wide_taps = jnp.concatenate(wide_taps, axis=0).astype(BF16)
    rest_taps = jnp.concatenate(rest_taps, axis=0).astype(BF16)[:, : taps - LANES]
    steps = []
    for u in range(3):
        steps.append(
            jnp.dot(wide_taps, cw[pl.ds(u * taps, LANES), :], preferred_element_type=F32)
            + jnp.dot(rest_taps, cw[pl.ds(u * taps + LANES, taps - LANES), :], preferred_element_type=F32)
        )
    for copy in pending:
        copy.wait_send()
    gain = gain_ref[...][None, :]
    decoded = []
    for cell in range(4):
        rows = slice(cell * 8, cell * 8 + 8)
        conv = steps[0][rows] + pltpu.roll(steps[1][rows], 7, 0) + pltpu.roll(steps[2][rows], 6, 0)
        square = jnp.sum(conv * conv, axis=1, keepdims=True) / conv.shape[1]
        scaled = conv * lax.rsqrt(square + 1e-6) * gain
        decoded.append(scaled / (1.0 + jnp.exp(-scaled)))
    for f in range(z.frames):
        for i in range(2):
            pair_of = [decoded[i * 2 + j][f : f + 1] for j in range(2)]
            dec_ref[f, i] = jnp.concatenate(pair_of, axis=0).astype(BF16)


def local(
    mesh, stream, queries, span_k, span_v, cache_k, cache_v, cache_age, history, out_weight,
    attn_gate, head_shift, head_scale, head_weight, latent_cache, conv_weight, rms_gain,
):
    queries, span_k, span_v = (t[:, :, 0] for t in (queries, span_k, span_v))
    out_weight, head_weight = out_weight.T, head_weight.T
    z = Sizes(mesh, queries, cache_k, out_weight)
    model, chan = z.model, conv_weight.shape[1]
    vmem = pl.BlockSpec(memory_space=pltpu.VMEM)
    hbm = pl.BlockSpec(memory_space=pl.ANY)
    half = z.all // 2
    dma = lambda *shape: pltpu.SemaphoreType.DMA(shape)
    out, dec = pl.pallas_call(
        functools.partial(kernel, z),
        out_shape=(
            jax.ShapeDtypeStruct((z.frames, model), BF16),
            jax.ShapeDtypeStruct((z.frames, 2, 2, chan), BF16),
        ),
        in_specs=[vmem] * 4 + [pl.BlockSpec(memory_space=pltpu.SMEM)] + [vmem] * 6 + [hbm] * 5,
        out_specs=(vmem, vmem),
        scratch_shapes=[
            pltpu.VMEM((z.chunks, z.all, z.wide), BF16),
            pltpu.VMEM((z.chunks, z.all, z.wide), BF16),
            pltpu.VMEM((z.chunks, z.all, z.wide + LANES), BF16),
            pltpu.VMEM((z.chunks, half, z.wide + LANES), BF16),
            pltpu.VMEM((z.chunks, half, z.wide + LANES), BF16),
            pltpu.VMEM((z.chunks, half, z.wide + LANES), BF16),
            pltpu.VMEM((z.halves * z.keys, z.lanes), BF16),
            pltpu.VMEM((z.halves * z.keys, z.lanes), BF16),
            pltpu.VMEM(out_weight.shape, BF16),
            pltpu.VMEM(head_weight.shape, BF16),
            pltpu.VMEM(conv_weight.shape, BF16),
            pltpu.VMEM((z.nhd, z.nsp * z.message, LANES), BF16),
            pltpu.VMEM((z.nhd, z.nsp * z.message, LANES), BF16),
            pltpu.VMEM((z.nsp * z.message, LANES), BF16),
            pltpu.VMEM((z.nsp * z.message, LANES), BF16),
            pltpu.VMEM((9, 16, LANES), BF16),
            pltpu.VMEM((16, LANES), BF16),
            pltpu.VMEM((16, LANES), F32),
            pltpu.VMEM((z.nsp * z.message, z.pieces * z.nsp * z.tp), BF16),
            pltpu.VMEM((z.pieces * z.nsp * 8, z.nsp * z.message), BF16),
            dma(2 * z.halves + 3),
            dma(2, z.chunks, z.nchip), dma(2, z.chunks, z.nchip),
            dma(2, z.chunks, z.nchip), dma(2, z.chunks, z.nchip),
            dma(2, z.chunks, z.nchip), dma(2, z.chunks, z.nchip),
            dma(z.chunks), dma(z.chunks),
            dma(z.chunks, z.nchip), dma(z.chunks, z.nchip),
            dma(z.nhd), dma(z.nhd),
            dma(z.nsp), dma(z.nsp),
            dma(9), dma(9),
        ],
        compiler_params=pltpu.CompilerParams(
            collective_id=0, has_side_effects=True, vmem_limit_bytes=56 * 1024 * 1024
        ),
        name="span_block",
    )(
        queries, span_k, span_v, cache_age, history, stream.reshape(z.frames, model),
        attn_gate[None], head_shift[None], head_scale[None], latent_cache, rms_gain,
        cache_k, cache_v, out_weight, head_weight, conv_weight,
    )
    return out.reshape(stream.shape), dec


def solution(mesh):
    placed = (
        P(None, "hd", "sp", None),
        P(None, None, "sp", "hd"),
        P(None, None, "sp", "hd"),
        P(None, None, "sp", "hd"),
        P("sp", "hd"),
        P("sp", "hd"),
        P("sp"),
        P(),
        P("hd", "sp"),
        P(),
        P(),
        P(),
        P(),
        P(None, "hd", "sp", None),
        P(),
        P(),
    )
    return jax.shard_map(
        functools.partial(local, mesh),
        mesh=mesh,
        in_specs=placed,
        out_specs=(P(None, "hd", "sp", None), P(None, "hd", "sp", None)),
        check_vma=False,
    )
```

```python
import functools
import math

import jax
import jax.numpy as jnp
from jax import lax
from jax.experimental import pallas as pl
from jax.experimental.pallas import tpu as pltpu
from jax.sharding import PartitionSpec as P

HDIM = 128
LANES = 128
MESH = pl.DeviceIdType.MESH
F32 = jnp.float32
BF16 = jnp.bfloat16


def up(value, unit):
    return -(-value // unit) * unit


class Sizes:
    def __init__(self, mesh, queries, cache_k, out_weight):
        self.nsp, self.nhd = mesh.shape["sp"], mesh.shape["hd"]
        self.nchip = self.nsp // 2
        self.frames, self.rows, self.width = queries.shape
        self.heads = self.width // HDIM
        self.own = self.rows // self.nhd
        self.tokens = self.frames * self.rows
        self.slot = up(self.own * self.frames, 4)
        self.tp = self.slot * self.nhd
        self.halves = 2 if self.tp % 16 and self.heads % 2 == 0 else 1
        if self.halves == 1:
            self.tp = up(self.tp, 16)
        self.block = self.halves * self.tp
        self.lanes = self.width // self.halves
        self.pairs = self.heads // self.halves
        self.chunks = 1 if self.pairs % 2 else 2
        self.chunk_pairs = self.pairs // self.chunks
        self.wide = self.lanes // self.chunks
        self.cache = cache_k.shape[0]
        self.keys = up(self.cache + up(self.tp, 16), LANES)
        self.span = self.keys - self.cache
        self.all = self.nsp * self.block
        self.part = out_weight.shape[0]
        self.pieces = -(-self.part // LANES)
        self.message = up(self.pieces * self.slot, 16)
        self.model = self.part * self.nsp

    def slots(self):
        for f in range(self.frames):
            for r in range(self.rows):
                yield (r // self.own) * self.slot + (r % self.own) * self.frames + f, f, r


def div(value, by):
    return value >> (by.bit_length() - 1) if by & (by - 1) == 0 else value // by


def mod(value, by):
    return value & (by - 1) if by & (by - 1) == 0 else value % by


def iota(shape, dim):
    return lax.broadcasted_iota(jnp.int32, shape, dim)


def merge_stats(stats):
    top = functools.reduce(jnp.maximum, stats)
    scales = [jnp.exp(s - top) for s in stats]
    total = functools.reduce(
        jnp.add, [s * pltpu.roll(a, 64, 1) for s, a in zip(stats, scales)]
    )
    return top, total, scales


def kernel(
    z, q_ref, k_ref, v_ref, age_ref, history_ref, stream_ref, gate_ref, shift_ref, scale_ref, latc_ref, gain_ref,
    ck_hbm, cv_hbm, w_hbm, hw_hbm, cw_hbm,
    so_ref, dec_ref,
    g, att, o, o_in, co, o_got, k2, v2, w, hw, cw, zs, z_got, h, r_got, near, msg, tmp, pick_out, pick_in, projected,
    local_sem, z_send, z_recv, x_send, x_recv, c_send, c_recv, sib_send, sib_recv, b_send, b_recv,
    hd_send, hd_recv, e_send, e_recv, n_send, n_recv,
):
    me, my = lax.axis_index("sp"), lax.axis_index("hd")
    core, chip = me % 2, me // 2
    sib = me + 1 - 2 * core
    nchip, block = z.nchip, z.block

    def peer(k):
        return (chip + k) % nchip

    def source(k):
        return (chip + nchip - k) % nchip

    far, side = nchip // 2, chip % 2

    def place(which_chip):
        return (which_chip % 2) * far + which_chip // 2

    def rows_of(which_core, which_chip):
        return pl.ds(pl.multiple_of((which_core * nchip + place(which_chip)) * block, block), block)

    def chip_rows(which_chip):
        return pl.ds(pl.multiple_of(place(which_chip) * block, block), block)

    def remote(src, dst, ssem, rsem, sp, hd):
        return pltpu.make_async_remote_copy(
            src_ref=src, dst_ref=dst, send_sem=ssem, recv_sem=rsem,
            device_id=(sp, hd), device_id_type=MESH,
        )

    def packed(ref):
        row = iota((z.tp, z.width), 0)
        out = jnp.zeros((z.tp, z.width), F32)
        for slot, f, r in z.slots():
            out = jnp.where(row == slot, ref[f, r : r + 1, :].astype(F32), out)
        return [out[:, i * z.lanes : (i + 1) * z.lanes] for i in range(z.halves)]

    near[...] = jnp.zeros_like(near)

    barrier = pltpu.get_barrier_semaphore()
    for k in range(1, z.nsp):
        pl.semaphore_signal(barrier, inc=1, device_id=((me + k) % z.nsp, my), device_id_type=MESH)
    for k in range(1, z.nhd):
        pl.semaphore_signal(barrier, inc=1, device_id=(me, (my + k) % z.nhd), device_id_type=MESH)

    def inside(dr, dc):
        ok = None
        for step, at, count in ((dr, my, z.nhd), (dc, me, z.nsp)):
            if step:
                here = (at + step >= 0) & (at + step < count)
                ok = here if ok is None else ok & here
        return ok

    greeted = z.nsp - 1 + z.nhd - 1
    for dr in (-1, 1):
        for dc in (-1, 1):

            @pl.when(inside(dr, dc))
            def _():
                pl.semaphore_signal(barrier, inc=1, device_id=(me + dc, my + dr), device_id_type=MESH)

            greeted = greeted + inside(dr, dc).astype(jnp.int32)
    loads = []

    def load(src, dst):
        copy = pltpu.make_async_copy(src, dst, local_sem.at[len(loads)])
        copy.start()
        loads.append(copy)

    for half in range(z.halves):
        cols = pl.ds(half * z.lanes, z.lanes)
        load(ck_hbm.at[:, cols], k2.at[pl.ds(half * z.keys, z.cache)])
        load(cv_hbm.at[:, cols], v2.at[pl.ds(half * z.keys, z.cache)])
    attention_loads = len(loads)
    load(w_hbm, w)
    load(hw_hbm, hw)
    load(cw_hbm, cw)

    mine_q = jnp.concatenate(packed(q_ref), axis=0).astype(BF16)
    g[rows_of(core, chip), :] = mine_q
    pl.semaphore_wait(barrier, greeted)

    partner = (chip + 1 - 2 * side) * 2 + core
    pending = []

    def distant(k):
        return (chip // 2 + far - k) % far

    def pass_on(buf, phase, rows, sems, slot, to):
        ssem, rsem = sems
        copy = remote(buf.at[rows], buf.at[rows], ssem.at[phase, slot], rsem.at[phase, slot], to, my)
        copy.start()
        pending.append(copy)
        return copy

    along, across, within = (z_send, z_recv), (x_send, x_recv), (c_send, c_recv)

    class Gather:
        def __init__(self, buf, phase):
            self.at = (buf, phase)
            mine = rows_of(core, chip)
            self.z = [
                pass_on(*self.at, mine, along, k, (((chip // 2 + k) % far) * 2 + side) * 2 + core)
                for k in range(1, far)
            ]
            self.x = [pass_on(*self.at, mine, across, 0, partner)]
            self.c = []

        def batch(self, which_side):
            rows = pl.ds(pl.multiple_of((core * 2 + which_side) * far * block, far * block), far * block)
            self.c.append(pass_on(*self.at, rows, within, len(self.c), sib))

        def relay(self):
            for k in range(1, far):
                self.z[k - 1].wait_recv()
                self.x.append(pass_on(*self.at, rows_of(core, distant(k) * 2 + side), across, k, partner))
            self.batch(side)
            for copy in self.x:
                copy.wait_recv()
            self.batch(1 - side)

        def finish(self):
            for copy in self.c:
                copy.wait_recv()

    asked = Gather(g, 0)
    for ref, buf in ((k_ref, k2), (v_ref, v2)):
        for half, part in enumerate(packed(ref)):
            if z.span > z.tp:
                part = jnp.concatenate([part, jnp.zeros((z.span - z.tp, z.lanes), F32)], axis=0)
            buf[pl.ds(half * z.keys + z.cache, z.span), :] = part.astype(BF16)
    out_rows, in_rows = z.nsp * z.message, z.nsp * z.tp
    out_at, in_at = iota((out_rows, in_rows), 0), iota((out_rows, in_rows), 1)
    out_sp, inner = div(out_at, z.message), mod(out_at, z.message)
    at_chip = mod(out_sp, 2) * nchip + mod(div(out_sp, 2), 2) * far + div(out_sp, 4)
    wanted = in_at == at_chip * z.tp + mod(inner, z.slot)
    for piece in range(z.pieces):
        picked = jnp.where(wanted & (div(inner, z.slot) == piece), 1.0, 0.0).astype(BF16)
        pick_out[:, pl.ds(piece * in_rows, in_rows)] = picked
    to_rows, from_rows = z.nsp * 8, z.nsp * z.message
    to_at, from_at = iota((to_rows, from_rows), 0), iota((to_rows, from_rows), 1)
    to_slot = mod(to_at, 8)
    wanted = from_at - div(to_at, 8) * z.message - to_slot
    for piece in range(z.pieces):
        picked = (wanted == piece * z.slot) & (to_slot < z.slot)
        pick_in[pl.ds(piece * to_rows, to_rows), :] = jnp.where(picked, 1.0, 0.0).astype(BF16)

    half_rows = nchip * block
    chunk = min(half_rows, 256)
    total_keys = z.halves * z.keys
    lane = iota((chunk, LANES), 1)
    scale = 1.0 / math.sqrt(HDIM)
    key = iota((1, z.keys), 1)
    live = jnp.where(age_ref[...][None, :] < history_ref[0], 1.0, 0.0).astype(F32)
    live = jnp.concatenate([live, jnp.zeros((1, z.span), F32)], axis=1)
    for slot, _, _ in z.slots():
        live = jnp.where(key == z.cache + slot, 1.0, live)
    bounds = [jnp.broadcast_to(live, (chunk, z.keys))] * z.halves
    if z.halves > 1:
        row_half = mod(div(iota((chunk, z.keys), 0), z.tp), z.halves)
        bounds = [jnp.where(row_half == half, b, 0.0) for half, b in enumerate(bounds)]
    mask = jnp.concatenate(bounds, axis=1) > 0.0
    ones = jnp.ones((total_keys, LANES), BF16)

    for copy in loads[:attention_loads]:
        copy.wait()
    asked.relay()

    def attend(which_core, ch):
        def step(at, carry):
            rows = pl.ds(pl.multiple_of(which_core * half_rows + at * chunk, chunk), chunk)
            stat_cols = pl.ds(z.wide, LANES)
            stats = jnp.zeros((chunk, LANES), F32)
            for j in range(z.chunk_pairs):
                near_cols = pl.ds(j * HDIM, HDIM)
                cols = pl.ds(ch * z.wide + j * HDIM, HDIM)
                scores = lax.dot_general(
                    g[rows, cols], k2[:, cols], (((1,), (1,)), ((), ())), preferred_element_type=F32
                )
                scores = jnp.where(mask, scores * scale, -1e30)
                top = jnp.max(scores, axis=1, keepdims=True).astype(BF16).astype(F32)
                weights = jnp.exp(scores - top).astype(BF16)
                out = jnp.dot(
                    weights, jnp.concatenate([v2[:, cols], ones], axis=1), preferred_element_type=F32
                )
                o[ch, rows, near_cols] = out[:, :HDIM].astype(BF16)
                stats = jnp.where(lane == j, top, jnp.where(lane == j + 64, out[:, HDIM:], stats))
            o[ch, rows, stat_cols] = stats.astype(BF16)
            return carry

        if half_rows == chunk:
            step(0, 0)
        else:
            lax.fori_loop(0, half_rows // chunk, step, 0)

    theirs = pl.ds(pl.multiple_of((1 - core) * half_rows, half_rows), half_rows)
    low = iota((block, LANES), 1) < 64

    def give(ch):
        copy = remote(o.at[ch, theirs], o_in.at[ch], sib_send.at[ch], sib_recv.at[ch], sib, my)
        copy.start()
        pending.append(copy)
        return copy

    def merge(ch, given):
        given.wait_recv()
        stat_cols = pl.ds(z.wide, LANES)
        copies = []
        for k in list(range(1, nchip)) + [0]:
            to = peer(k)
            mine, rows = rows_of(core, to), chip_rows(to)
            top, total, (a, b) = merge_stats(
                [o[ch, mine, stat_cols].astype(F32), o_in[ch, rows, stat_cols].astype(F32)]
            )
            dst, at = (co, rows) if k else (o_got, chip_rows(chip))
            dst[ch, at, stat_cols] = jnp.where(low, top, total).astype(BF16)
            for j in range(z.chunk_pairs):
                cols = pl.ds(j * HDIM, HDIM)
                merged = (
                    o[ch, mine, cols].astype(F32) * a[:, j : j + 1]
                    + o_in[ch, rows, cols].astype(F32) * b[:, j : j + 1]
                )
                dst[ch, at, cols] = merged.astype(BF16)
            if k:
                copy = remote(co.at[ch, rows], o_got.at[ch, chip_rows(chip)], b_send.at[ch, k], b_recv.at[ch, k],
                              to * 2 + core, my)
                copy.start()
                copies.append(copy)
        pending.extend(copies)
        return copies

    def settle(ch, copies):
        for copy in copies:
            copy.wait_recv()
        parts = [pl.ds(i * block, block) for i in range(nchip)]
        top, total, scales = merge_stats([o_got[ch, p, pl.ds(z.wide, LANES)].astype(F32) for p in parts])
        inverse = pltpu.roll(1.0 / jnp.where(low, 1.0, total), 64, 1)
        for j in range(z.chunk_pairs):
            cols = pl.ds(j * HDIM, HDIM)
            terms = [o_got[ch, p, cols].astype(F32) * s[:, j : j + 1] for p, s in zip(parts, scales)]
            summed = functools.reduce(jnp.add, terms)
            cols = pl.ds(ch * z.wide + j * HDIM, HDIM)
            att[rows_of(core, chip), cols] = (summed * inverse[:, j : j + 1]).astype(BF16)

    for ch in range(z.chunks):
        attend(core, ch)
    asked.finish()
    given = []
    for ch in range(z.chunks):
        attend(1 - core, ch)
        given.append(give(ch))
    partials = [merge(ch, given[ch]) for ch in range(z.chunks)]
    for ch in range(z.chunks):
        settle(ch, partials[ch])
    shared = Gather(att, 1)

    def project(which_core):
        part_rows = nchip * z.tp
        tokens = att[pl.ds(pl.multiple_of(which_core * half_rows, half_rows), half_rows), :]
        total = None
        for half in range(z.halves):
            term = lax.dot_general(
                tokens, w[:, pl.ds(half * z.lanes, z.lanes)], (((1,), (1,)), ((), ())),
                preferred_element_type=F32,
            )
            term = term.reshape(nchip, z.halves, z.tp, z.part)[:, half]
            total = term if total is None else total + term
        rows = pl.ds(pl.multiple_of(which_core * part_rows, part_rows), part_rows)
        projected[rows, :] = total.reshape(part_rows, z.part)

    for copy in loads[attention_loads:]:
        copy.wait()
    shared.relay()
    project(core)
    shared.finish()
    project(1 - core)
    proj = projected[...]
    wide = z.pieces * LANES
    if wide > z.part:
        proj = jnp.concatenate([proj, jnp.zeros((in_rows, wide - z.part), F32)], axis=1)
    owned = []
    for owner in range(z.nhd):
        turned = pltpu.roll(proj, in_rows - owner * z.slot, 0) if owner else proj
        turned = turned.astype(BF16)
        owned.append(
            jnp.concatenate([turned[:, i * LANES : (i + 1) * LANES] for i in range(z.pieces)], axis=0)
        )
    moved = jnp.dot(pick_out[...], jnp.concatenate(owned, axis=1), preferred_element_type=F32).astype(BF16)
    for owner in range(z.nhd):
        zs[owner] = moved[:, owner * LANES : (owner + 1) * LANES]

    swaps = []
    for k in range(1, z.nhd):
        to = (my + k) % z.nhd
        copy = remote(zs.at[to], z_got.at[my], hd_send.at[k], hd_recv.at[k], me, to)
        copy.start()
        swaps.append(copy)
    summed = zs[my].astype(F32)
    for k in range(1, z.nhd):
        swaps[k - 1].wait_recv()
        summed = summed + z_got[(my + z.nhd - k) % z.nhd].astype(F32)
    h[...] = summed.astype(BF16)

    def message_rows(at):
        return pl.ds(pl.multiple_of(at * z.message, z.message), z.message)

    spread = []
    for k in range(1, z.nsp):
        to = (me + k) % z.nsp
        copy = remote(h.at[message_rows(to)], r_got.at[message_rows(me)], e_send.at[k], e_recv.at[k], to, my)
        copy.start()
        spread.append(copy)
    r_got[message_rows(me), :] = h[message_rows(me), :]
    pending.extend(swaps)
    pending.extend(spread)
    for copy in spread:
        copy.wait_recv()

    picked = jnp.dot(pick_in[...], r_got[...], preferred_element_type=F32)
    by_piece = [picked[i * to_rows : (i + 1) * to_rows] for i in range(z.pieces)]
    lane8 = iota((8, LANES), 1)
    row8 = iota((8, LANES), 0)
    tiles = []
    for tile in range(z.model // LANES):
        value = jnp.zeros((8, LANES), F32)
        begin = tile * LANES
        for s in range(begin // z.part, (begin + LANES - 1) // z.part + 1):
            for piece in range(z.pieces):
                low_at = s * z.part + piece * LANES
                high_at = min(low_at + LANES, (s + 1) * z.part)
                a, b = max(low_at, begin), min(high_at, begin + LANES)
                if a >= b:
                    continue
                cell = by_piece[piece][s * 8 : (s + 1) * 8]
                if (low_at - begin) % LANES:
                    cell = pltpu.roll(cell, (low_at - begin) % LANES, 1)
                value = jnp.where((lane8 >= a - begin) & (lane8 < b - begin), cell, value)
        cols = pl.ds(begin, LANES)
        base_value = jnp.zeros((8, LANES), F32)
        for f in range(z.frames):
            base_value = jnp.where(row8 == f, stream_ref[f : f + 1, cols].astype(F32), base_value)
        value = base_value + gate_ref[:, cols] * value
        rounded = value.astype(BF16)
        so_ref[:, cols] = rounded[: z.frames]
        value = rounded.astype(F32)
        tiles.append(value)
    mean = jnp.sum(functools.reduce(jnp.add, tiles), axis=1, keepdims=True) / z.model
    centred = [t - mean for t in tiles]
    variance = jnp.sum(functools.reduce(jnp.add, [t * t for t in centred]), axis=1, keepdims=True) / z.model
    root = lax.rsqrt(variance + 1e-6)
    normed = []
    for tile, t in enumerate(centred):
        cols = pl.ds(tile * LANES, LANES)
        normed.append(t * root * (1.0 + scale_ref[:, cols]) + shift_ref[:, cols])
    normed = jnp.concatenate(normed, axis=1)
    normed = jnp.concatenate([normed, jnp.zeros_like(normed)], axis=0).astype(BF16)
    patch = lax.dot_general(
        normed, hw[...], (((1,), (1,)), ((), ())), preferred_element_type=F32
    )
    cells = patch.shape[1]
    past = latc_ref.shape[0]
    tmp[...] = jnp.zeros_like(tmp)
    chan = cells // 4
    for f in range(past):
        for a in range(2):
            for b in range(2):
                at = (a * 2 + b) * chan
                tmp[f : f + 1, at : at + chan] = latc_ref[f, a, b : b + 1, :].astype(F32)
    tmp[past : past + z.frames, 0:cells] = patch[0 : z.frames]
    msg[...] = tmp[...].astype(BF16)

    order = [(dr, dc) for dr in (-1, 0, 1) for dc in (-1, 0, 1) if (dr, dc) != (0, 0)]

    def halo(dr, dc):
        at = (dr + 1) * 3 + dc + 1
        return remote(msg, near.at[8 - at], n_send.at[at], n_recv.at[8 - at], me + dc, my + dr)

    for dr, dc in order:

        @pl.when(inside(dr, dc))
        def _():
            halo(dr, dc).start()

    near[4] = msg[...]
    for dr, dc in order:

        @pl.when(inside(dr, dc))
        def _():
            copy = halo(dr, dc)
            copy.wait_send()
            pltpu.make_async_remote_copy(
                src_ref=msg, dst_ref=near.at[(dr + 1) * 3 + dc + 1],
                send_sem=n_send.at[(dr + 1) * 3 + dc + 1], recv_sem=n_recv.at[(dr + 1) * 3 + dc + 1],
                device_id=(me + dc, my + dr), device_id_type=MESH,
            ).wait_recv()

    around = [near[i].astype(F32)[0:8] for i in range(9)]
    taps = 9 * chan
    wide_taps, rest_taps = [], []
    for i in range(2):
        for j in range(2):
            parts = [jnp.zeros((8, LANES), F32), jnp.zeros((8, LANES), F32)]
            for v in range(3):
                for u in range(3):
                    ri, ci = i + v - 1, j + u - 1
                    at = (ri // 2 + 1) * 3 + ci // 2 + 1
                    src = ((ri % 2) * 2 + ci % 2) * chan
                    to = (v * 3 + u) * chan
                    shift = (to - src) % LANES
                    cell = pltpu.roll(around[at], shift, 1) if shift else around[at]
                    inner_at = to % LANES
                    parts[to // LANES] = jnp.where(
                        (lane8 >= inner_at) & (lane8 < inner_at + chan), cell, parts[to // LANES]
                    )
            wide_taps.append(parts[0])
            rest_taps.append(parts[1])
    wide_taps = jnp.concatenate(wide_taps, axis=0).astype(BF16)
    rest_taps = jnp.concatenate(rest_taps, axis=0).astype(BF16)[:, : taps - LANES]
    steps = []
    for u in range(3):
        steps.append(
            jnp.dot(wide_taps, cw[pl.ds(u * taps, LANES), :], preferred_element_type=F32)
            + jnp.dot(rest_taps, cw[pl.ds(u * taps + LANES, taps - LANES), :], preferred_element_type=F32)
        )
    for copy in pending:
        copy.wait_send()
    gain = gain_ref[...][None, :]
    decoded = []
    for cell in range(4):
        rows = slice(cell * 8, cell * 8 + 8)
        conv = steps[0][rows] + pltpu.roll(steps[1][rows], 7, 0) + pltpu.roll(steps[2][rows], 6, 0)
        square = jnp.sum(conv * conv, axis=1, keepdims=True) / conv.shape[1]
        scaled = conv * lax.rsqrt(square + 1e-6) * gain
        decoded.append(scaled / (1.0 + jnp.exp(-scaled)))
    for f in range(z.frames):
        for i in range(2):
            pair_of = [decoded[i * 2 + j][f : f + 1] for j in range(2)]
            dec_ref[f, i] = jnp.concatenate(pair_of, axis=0).astype(BF16)


def local(
    mesh, stream, queries, span_k, span_v, cache_k, cache_v, cache_age, history, out_weight,
    attn_gate, head_shift, head_scale, head_weight, latent_cache, conv_weight, rms_gain,
):
    queries, span_k, span_v = (t[:, :, 0] for t in (queries, span_k, span_v))
    out_weight, head_weight = out_weight.T, head_weight.T
    z = Sizes(mesh, queries, cache_k, out_weight)
    model, chan = z.model, conv_weight.shape[1]
    vmem = pl.BlockSpec(memory_space=pltpu.VMEM)
    hbm = pl.BlockSpec(memory_space=pl.ANY)
    half = z.all // 2
    dma = lambda *shape: pltpu.SemaphoreType.DMA(shape)
    out, dec = pl.pallas_call(
        functools.partial(kernel, z),
        out_shape=(
            jax.ShapeDtypeStruct((z.frames, model), BF16),
            jax.ShapeDtypeStruct((z.frames, 2, 2, chan), BF16),
        ),
        in_specs=[vmem] * 4 + [pl.BlockSpec(memory_space=pltpu.SMEM)] + [vmem] * 6 + [hbm] * 5,
        out_specs=(vmem, vmem),
        scratch_shapes=[
            pltpu.VMEM((z.all, z.lanes), BF16),
            pltpu.VMEM((z.all, z.lanes), BF16),
            pltpu.VMEM((z.chunks, z.all, z.wide + LANES), BF16),
            pltpu.VMEM((z.chunks, half, z.wide + LANES), BF16),
            pltpu.VMEM((z.chunks, half, z.wide + LANES), BF16),
            pltpu.VMEM((z.chunks, half, z.wide + LANES), BF16),
            pltpu.VMEM((z.halves * z.keys, z.lanes), BF16),
            pltpu.VMEM((z.halves * z.keys, z.lanes), BF16),
            pltpu.VMEM(out_weight.shape, BF16),
            pltpu.VMEM(head_weight.shape, BF16),
            pltpu.VMEM(conv_weight.shape, BF16),
            pltpu.VMEM((z.nhd, z.nsp * z.message, LANES), BF16),
            pltpu.VMEM((z.nhd, z.nsp * z.message, LANES), BF16),
            pltpu.VMEM((z.nsp * z.message, LANES), BF16),
            pltpu.VMEM((z.nsp * z.message, LANES), BF16),
            pltpu.VMEM((9, 16, LANES), BF16),
            pltpu.VMEM((16, LANES), BF16),
            pltpu.VMEM((16, LANES), F32),
            pltpu.VMEM((z.nsp * z.message, z.pieces * z.nsp * z.tp), BF16),
            pltpu.VMEM((z.pieces * z.nsp * 8, z.nsp * z.message), BF16),
            pltpu.VMEM((z.nsp * z.tp, z.part), F32),
            dma(2 * z.halves + 3),
            dma(2, z.nchip), dma(2, z.nchip), dma(2, z.nchip), dma(2, z.nchip), dma(2, 2), dma(2, 2),
            dma(z.chunks), dma(z.chunks),
            dma(z.chunks, z.nchip), dma(z.chunks, z.nchip),
            dma(z.nhd), dma(z.nhd),
            dma(z.nsp), dma(z.nsp),
            dma(9), dma(9),
        ],
        compiler_params=pltpu.CompilerParams(
            collective_id=0, has_side_effects=True, vmem_limit_bytes=56 * 1024 * 1024
        ),
        name="span_block",
    )(
        queries, span_k, span_v, cache_age, history, stream.reshape(z.frames, model),
        attn_gate[None], head_shift[None], head_scale[None], latent_cache, rms_gain,
        cache_k, cache_v, out_weight, head_weight, conv_weight,
    )
    return out.reshape(stream.shape), dec


def solution(mesh):
    placed = (
        P(None, "hd", "sp", None),
        P(None, None, "sp", "hd"),
        P(None, None, "sp", "hd"),
        P(None, None, "sp", "hd"),
        P("sp", "hd"),
        P("sp", "hd"),
        P("sp"),
        P(),
        P("hd", "sp"),
        P(),
        P(),
        P(),
        P(),
        P(None, "hd", "sp", None),
        P(),
        P(),
    )
    return jax.shard_map(
        functools.partial(local, mesh),
        mesh=mesh,
        in_specs=placed,
        out_specs=(P(None, "hd", "sp", None), P(None, "hd", "sp", None)),
        check_vma=False,
    )
```

```python
import functools
import math

import jax
import jax.numpy as jnp
from jax import lax
from jax.experimental import pallas as pl
from jax.experimental.pallas import tpu as pltpu
from jax.sharding import PartitionSpec as P

HDIM = 128
LANES = 128
MESH = pl.DeviceIdType.MESH
F32 = jnp.float32
BF16 = jnp.bfloat16


def up(value, unit):
    return -(-value // unit) * unit


class Sizes:
    def __init__(self, mesh, queries, cache_k, out_weight):
        self.nsp, self.nhd = mesh.shape["sp"], mesh.shape["hd"]
        self.nchip = self.nsp // 2
        self.frames, self.rows, self.width = queries.shape
        self.heads = self.width // HDIM
        self.own = self.rows // self.nhd
        self.tokens = self.frames * self.rows
        self.slot = up(self.own * self.frames, 4)
        self.tp = self.slot * self.nhd
        self.halves = 2 if self.tp % 16 and self.heads % 2 == 0 else 1
        if self.halves == 1:
            self.tp = up(self.tp, 16)
        self.block = self.halves * self.tp
        self.lanes = self.width // self.halves
        self.pairs = self.heads // self.halves
        self.chunks = 1 if self.pairs % 2 else 2
        self.chunk_pairs = self.pairs // self.chunks
        self.wide = self.lanes // self.chunks
        self.cache = cache_k.shape[0]
        self.keys = up(self.cache + up(self.tp, 16), LANES)
        self.span = self.keys - self.cache
        self.all = self.nsp * self.block
        self.part = out_weight.shape[0]
        self.pieces = -(-self.part // LANES)
        self.message = up(self.pieces * self.slot, 16)
        self.model = self.part * self.nsp

    def slots(self):
        for f in range(self.frames):
            for r in range(self.rows):
                yield (r // self.own) * self.slot + (r % self.own) * self.frames + f, f, r


def div(value, by):
    return value >> (by.bit_length() - 1) if by & (by - 1) == 0 else value // by


def mod(value, by):
    return value & (by - 1) if by & (by - 1) == 0 else value % by


def iota(shape, dim):
    return lax.broadcasted_iota(jnp.int32, shape, dim)


def merge_stats(stats):
    top = functools.reduce(jnp.maximum, stats)
    scales = [jnp.exp(s - top) for s in stats]
    total = functools.reduce(
        jnp.add, [s * pltpu.roll(a, 64, 1) for s, a in zip(stats, scales)]
    )
    return top, total, scales


def kernel(
    z, q_ref, k_ref, v_ref, age_ref, history_ref, stream_ref, gate_ref, shift_ref, scale_ref, latc_ref, gain_ref,
    ck_hbm, cv_hbm, w_hbm, hw_hbm, cw_hbm,
    so_ref, dec_ref,
    g, att, o, o_in, co, o_got, k2, v2, w, hw, cw, zs, z_got, h, r_got, near, msg, tmp, pick_out, pick_in, projected,
    local_sem, z_send, z_recv, x_send, x_recv, c_send, c_recv, sib_send, sib_recv, b_send, b_recv,
    hd_send, hd_recv, e_send, e_recv, n_send, n_recv,
):
    me, my = lax.axis_index("sp"), lax.axis_index("hd")
    core, chip = me % 2, me // 2
    sib = me + 1 - 2 * core
    nchip, block = z.nchip, z.block

    far, side = nchip // 2, chip % 2

    def place(which_chip):
        return (which_chip % 2) * far + which_chip // 2

    def rows_of(which_core, which_chip):
        return pl.ds(pl.multiple_of((which_core * nchip + place(which_chip)) * block, block), block)

    def chip_rows(which_chip):
        return pl.ds(pl.multiple_of(place(which_chip) * block, block), block)

    def remote(src, dst, ssem, rsem, sp, hd):
        return pltpu.make_async_remote_copy(
            src_ref=src, dst_ref=dst, send_sem=ssem, recv_sem=rsem,
            device_id=(sp, hd), device_id_type=MESH,
        )

    def packed(ref):
        row = iota((z.tp, z.width), 0)
        out = jnp.zeros((z.tp, z.width), F32)
        for slot, f, r in z.slots():
            out = jnp.where(row == slot, ref[f, r : r + 1, :].astype(F32), out)
        return [out[:, i * z.lanes : (i + 1) * z.lanes] for i in range(z.halves)]

    near[...] = jnp.zeros_like(near)

    barrier = pltpu.get_barrier_semaphore()
    for k in range(1, z.nsp):
        pl.semaphore_signal(barrier, inc=1, device_id=((me + k) % z.nsp, my), device_id_type=MESH)
    for k in range(1, z.nhd):
        pl.semaphore_signal(barrier, inc=1, device_id=(me, (my + k) % z.nhd), device_id_type=MESH)

    def inside(dr, dc):
        ok = None
        for step, at, count in ((dr, my, z.nhd), (dc, me, z.nsp)):
            if step:
                here = (at + step >= 0) & (at + step < count)
                ok = here if ok is None else ok & here
        return ok

    greeted = z.nsp - 1 + z.nhd - 1
    for dr in (-1, 1):
        for dc in (-1, 1):

            @pl.when(inside(dr, dc))
            def _():
                pl.semaphore_signal(barrier, inc=1, device_id=(me + dc, my + dr), device_id_type=MESH)

            greeted = greeted + inside(dr, dc).astype(jnp.int32)
    loads = []

    def load(src, dst):
        copy = pltpu.make_async_copy(src, dst, local_sem.at[len(loads)])
        copy.start()
        loads.append(copy)

    for half in range(z.halves):
        cols = pl.ds(half * z.lanes, z.lanes)
        load(ck_hbm.at[:, cols], k2.at[pl.ds(half * z.keys, z.cache)])
        load(cv_hbm.at[:, cols], v2.at[pl.ds(half * z.keys, z.cache)])
    attention_loads = len(loads)
    load(w_hbm, w)
    load(hw_hbm, hw)
    load(cw_hbm, cw)

    mine_q = jnp.concatenate(packed(q_ref), axis=0).astype(BF16)
    g[rows_of(core, chip), :] = mine_q
    pl.semaphore_wait(barrier, greeted)

    partner = (chip + 1 - 2 * side) * 2 + core
    pending = []

    def distant(k):
        return (chip // 2 + far - k) % far

    def pass_on(buf, phase, rows, sems, slot, to):
        ssem, rsem = sems
        copy = remote(buf.at[rows], buf.at[rows], ssem.at[phase, slot], rsem.at[phase, slot], to, my)
        copy.start()
        pending.append(copy)
        return copy

    along, across, within = (z_send, z_recv), (x_send, x_recv), (c_send, c_recv)

    class Gather:
        def __init__(self, buf, phase):
            self.at = (buf, phase)
            mine = rows_of(core, chip)
            self.z = [
                pass_on(*self.at, mine, along, k, (((chip // 2 + k) % far) * 2 + side) * 2 + core)
                for k in range(1, far)
            ]
            self.x = [pass_on(*self.at, mine, across, 0, partner)]
            self.c = []

        def batch(self, which_side):
            rows = pl.ds(pl.multiple_of((core * 2 + which_side) * far * block, far * block), far * block)
            self.c.append(pass_on(*self.at, rows, within, len(self.c), sib))

        def relay(self):
            for k in range(1, far):
                self.z[k - 1].wait_recv()
                self.x.append(pass_on(*self.at, rows_of(core, distant(k) * 2 + side), across, k, partner))
            self.batch(side)
            for copy in self.x:
                copy.wait_recv()
            self.batch(1 - side)

        def finish(self):
            for copy in self.c:
                copy.wait_recv()

    asked = Gather(g, 0)
    for ref, buf in ((k_ref, k2), (v_ref, v2)):
        for half, part in enumerate(packed(ref)):
            if z.span > z.tp:
                part = jnp.concatenate([part, jnp.zeros((z.span - z.tp, z.lanes), F32)], axis=0)
            buf[pl.ds(half * z.keys + z.cache, z.span), :] = part.astype(BF16)
    out_rows, in_rows = z.nsp * z.message, z.nsp * z.tp
    out_at, in_at = iota((out_rows, in_rows), 0), iota((out_rows, in_rows), 1)
    out_sp, inner = div(out_at, z.message), mod(out_at, z.message)
    at_chip = mod(out_sp, 2) * nchip + mod(div(out_sp, 2), 2) * far + div(out_sp, 4)
    wanted = in_at == at_chip * z.tp + mod(inner, z.slot)
    for piece in range(z.pieces):
        picked = jnp.where(wanted & (div(inner, z.slot) == piece), 1.0, 0.0).astype(BF16)
        pick_out[:, pl.ds(piece * in_rows, in_rows)] = picked
    to_rows, from_rows = z.nsp * 8, z.nsp * z.message
    to_at, from_at = iota((to_rows, from_rows), 0), iota((to_rows, from_rows), 1)
    to_slot = mod(to_at, 8)
    wanted = from_at - div(to_at, 8) * z.message - to_slot
    for piece in range(z.pieces):
        picked = (wanted == piece * z.slot) & (to_slot < z.slot)
        pick_in[pl.ds(piece * to_rows, to_rows), :] = jnp.where(picked, 1.0, 0.0).astype(BF16)

    half_rows = nchip * block
    chunk = min(half_rows, 256)
    total_keys = z.halves * z.keys
    lane = iota((chunk, LANES), 1)
    scale = 1.0 / math.sqrt(HDIM)
    key = iota((1, z.keys), 1)
    live = jnp.where(age_ref[...][None, :] < history_ref[0], 1.0, 0.0).astype(F32)
    live = jnp.concatenate([live, jnp.zeros((1, z.span), F32)], axis=1)
    for slot, _, _ in z.slots():
        live = jnp.where(key == z.cache + slot, 1.0, live)
    bounds = [jnp.broadcast_to(live, (chunk, z.keys))] * z.halves
    if z.halves > 1:
        row_half = mod(div(iota((chunk, z.keys), 0), z.tp), z.halves)
        bounds = [jnp.where(row_half == half, b, 0.0) for half, b in enumerate(bounds)]
    mask = jnp.concatenate(bounds, axis=1) > 0.0
    ones = jnp.ones((total_keys, LANES), BF16)

    for copy in loads[:attention_loads]:
        copy.wait()
    asked.relay()

    def attend(which_core, ch):
        def step(at, carry):
            rows = pl.ds(pl.multiple_of(which_core * half_rows + at * chunk, chunk), chunk)
            stats = jnp.zeros((chunk, LANES), F32)
            outs = []
            for j in range(z.chunk_pairs):
                cols = pl.ds(ch * z.wide + j * HDIM, HDIM)
                scores = lax.dot_general(
                    g[rows, cols], k2[:, cols], (((1,), (1,)), ((), ())), preferred_element_type=F32
                )
                scores = jnp.where(mask, scores * scale, -1e30)
                top = jnp.max(scores, axis=1, keepdims=True).astype(BF16).astype(F32)
                weights = jnp.exp(scores - top).astype(BF16)
                out = jnp.dot(
                    weights, jnp.concatenate([v2[:, cols], ones], axis=1), preferred_element_type=F32
                )
                outs.append(out[:, :HDIM].astype(BF16))
                stats = jnp.where(lane == j, top, jnp.where(lane == j + 64, out[:, HDIM:], stats))
            o[ch, rows, :] = jnp.concatenate(outs + [stats.astype(BF16)], axis=1)
            return carry

        if half_rows == chunk:
            step(0, 0)
        else:
            lax.fori_loop(0, half_rows // chunk, step, 0)

    theirs = pl.ds(pl.multiple_of((1 - core) * half_rows, half_rows), half_rows)
    low = iota((block, LANES), 1) < 64

    def give(ch):
        copy = remote(o.at[ch, theirs], o_in.at[ch], sib_send.at[ch], sib_recv.at[ch], sib, my)
        copy.start()
        pending.append(copy)
        return copy

    def merge(ch, given):
        given.wait_recv()
        stat_cols = pl.ds(z.wide, LANES)
        group = far * block
        group_low = iota((group, LANES), 1) < 64
        copies = []
        for across_side in (1, 0):
            to_side = (side + across_side) % 2
            rows = pl.ds(pl.multiple_of(to_side * group, group), group)
            mine = pl.ds(pl.multiple_of(core * half_rows + to_side * group, group), group)
            top, total, (a, b) = merge_stats(
                [o[ch, mine, stat_cols].astype(F32), o_in[ch, rows, stat_cols].astype(F32)]
            )
            merged = []
            for j in range(z.chunk_pairs):
                cols = pl.ds(j * HDIM, HDIM)
                value = (
                    o[ch, mine, cols].astype(F32) * a[:, j : j + 1]
                    + o_in[ch, rows, cols].astype(F32) * b[:, j : j + 1]
                )
                merged.append(value.astype(BF16))
            merged.append(jnp.where(group_low, top, total).astype(BF16))
            co[ch, rows, :] = jnp.concatenate(merged, axis=1)
            for k in range(far):
                if k == 0 and across_side == 0:
                    continue
                to = ((chip // 2 + k) % far) * 2 + to_side
                slot = across_side * far + k
                copy = remote(co.at[ch, chip_rows(to)], o_got.at[ch, chip_rows(chip)],
                              b_send.at[ch, slot], b_recv.at[ch, slot], to * 2 + core, my)
                copy.start()
                copies.append(copy)
        o_got[ch, chip_rows(chip), :] = co[ch, chip_rows(chip), :]
        pending.extend(copies)
        return copies

    def settle(ch, copies):
        for copy in copies:
            copy.wait_recv()
        parts = [pl.ds(i * block, block) for i in range(nchip)]
        top, total, scales = merge_stats([o_got[ch, p, pl.ds(z.wide, LANES)].astype(F32) for p in parts])
        done = []
        inverse = pltpu.roll(1.0 / jnp.where(low, 1.0, total), 64, 1)
        for j in range(z.chunk_pairs):
            cols = pl.ds(j * HDIM, HDIM)
            terms = [o_got[ch, p, cols].astype(F32) * s[:, j : j + 1] for p, s in zip(parts, scales)]
            summed = functools.reduce(jnp.add, terms)
            done.append((summed * inverse[:, j : j + 1]).astype(BF16))
        att[rows_of(core, chip), pl.ds(ch * z.wide, z.wide)] = jnp.concatenate(done, axis=1)

    for ch in range(z.chunks):
        attend(core, ch)
    asked.finish()
    given = []
    for ch in range(z.chunks):
        attend(1 - core, ch)
        given.append(give(ch))
    partials = [merge(ch, given[ch]) for ch in range(z.chunks)]
    for ch in range(z.chunks):
        settle(ch, partials[ch])
    shared = Gather(att, 1)

    def project(which_core):
        part_rows = nchip * z.tp
        tokens = att[pl.ds(pl.multiple_of(which_core * half_rows, half_rows), half_rows), :]
        total = None
        for half in range(z.halves):
            term = lax.dot_general(
                tokens, w[:, pl.ds(half * z.lanes, z.lanes)], (((1,), (1,)), ((), ())),
                preferred_element_type=F32,
            )
            term = term.reshape(nchip, z.halves, z.tp, z.part)[:, half]
            total = term if total is None else total + term
        rows = pl.ds(pl.multiple_of(which_core * part_rows, part_rows), part_rows)
        projected[rows, :] = total.reshape(part_rows, z.part)

    for copy in loads[attention_loads:]:
        copy.wait()
    shared.relay()
    project(core)
    shared.finish()
    project(1 - core)
    proj = projected[...]
    wide = z.pieces * LANES
    if wide > z.part:
        proj = jnp.concatenate([proj, jnp.zeros((in_rows, wide - z.part), F32)], axis=1)
    owned = []
    for owner in range(z.nhd):
        turned = pltpu.roll(proj, in_rows - owner * z.slot, 0) if owner else proj
        turned = turned.astype(BF16)
        owned.append(
            jnp.concatenate([turned[:, i * LANES : (i + 1) * LANES] for i in range(z.pieces)], axis=0)
        )
    moved = jnp.dot(pick_out[...], jnp.concatenate(owned, axis=1), preferred_element_type=F32).astype(BF16)
    for owner in range(z.nhd):
        zs[owner] = moved[:, owner * LANES : (owner + 1) * LANES]

    swaps = []
    for k in range(1, z.nhd):
        to = (my + k) % z.nhd
        copy = remote(zs.at[to], z_got.at[my], hd_send.at[k], hd_recv.at[k], me, to)
        copy.start()
        swaps.append(copy)
    summed = zs[my].astype(F32)
    for k in range(1, z.nhd):
        swaps[k - 1].wait_recv()
        summed = summed + z_got[(my + z.nhd - k) % z.nhd].astype(F32)
    h[...] = summed.astype(BF16)

    def message_rows(at):
        return pl.ds(pl.multiple_of(at * z.message, z.message), z.message)

    spread = []
    for k in range(1, z.nsp):
        to = (me + k) % z.nsp
        copy = remote(h.at[message_rows(to)], r_got.at[message_rows(me)], e_send.at[k], e_recv.at[k], to, my)
        copy.start()
        spread.append(copy)
    r_got[message_rows(me), :] = h[message_rows(me), :]
    pending.extend(swaps)
    pending.extend(spread)
    for copy in spread:
        copy.wait_recv()

    picked = jnp.dot(pick_in[...], r_got[...], preferred_element_type=F32)
    by_piece = [picked[i * to_rows : (i + 1) * to_rows] for i in range(z.pieces)]
    lane8 = iota((8, LANES), 1)
    row8 = iota((8, LANES), 0)
    tiles = []
    for tile in range(z.model // LANES):
        value = jnp.zeros((8, LANES), F32)
        begin = tile * LANES
        for s in range(begin // z.part, (begin + LANES - 1) // z.part + 1):
            for piece in range(z.pieces):
                low_at = s * z.part + piece * LANES
                high_at = min(low_at + LANES, (s + 1) * z.part)
                a, b = max(low_at, begin), min(high_at, begin + LANES)
                if a >= b:
                    continue
                cell = by_piece[piece][s * 8 : (s + 1) * 8]
                if (low_at - begin) % LANES:
                    cell = pltpu.roll(cell, (low_at - begin) % LANES, 1)
                value = jnp.where((lane8 >= a - begin) & (lane8 < b - begin), cell, value)
        cols = pl.ds(begin, LANES)
        base_value = jnp.zeros((8, LANES), F32)
        for f in range(z.frames):
            base_value = jnp.where(row8 == f, stream_ref[f : f + 1, cols].astype(F32), base_value)
        value = base_value + gate_ref[:, cols] * value
        rounded = value.astype(BF16)
        so_ref[:, cols] = rounded[: z.frames]
        value = rounded.astype(F32)
        tiles.append(value)
    mean = jnp.sum(functools.reduce(jnp.add, tiles), axis=1, keepdims=True) / z.model
    centred = [t - mean for t in tiles]
    variance = jnp.sum(functools.reduce(jnp.add, [t * t for t in centred]), axis=1, keepdims=True) / z.model
    root = lax.rsqrt(variance + 1e-6)
    normed = []
    for tile, t in enumerate(centred):
        cols = pl.ds(tile * LANES, LANES)
        normed.append(t * root * (1.0 + scale_ref[:, cols]) + shift_ref[:, cols])
    normed = jnp.concatenate(normed, axis=1)
    normed = jnp.concatenate([normed, jnp.zeros_like(normed)], axis=0).astype(BF16)
    patch = lax.dot_general(
        normed, hw[...], (((1,), (1,)), ((), ())), preferred_element_type=F32
    )
    cells = patch.shape[1]
    past = latc_ref.shape[0]
    tmp[...] = jnp.zeros_like(tmp)
    chan = cells // 4
    for f in range(past):
        for a in range(2):
            for b in range(2):
                at = (a * 2 + b) * chan
                tmp[f : f + 1, at : at + chan] = latc_ref[f, a, b : b + 1, :].astype(F32)
    tmp[past : past + z.frames, 0:cells] = patch[0 : z.frames]
    msg[...] = tmp[...].astype(BF16)

    order = [(dr, dc) for dr in (-1, 0, 1) for dc in (-1, 0, 1) if (dr, dc) != (0, 0)]

    def halo(dr, dc):
        at = (dr + 1) * 3 + dc + 1
        return remote(msg, near.at[8 - at], n_send.at[at], n_recv.at[8 - at], me + dc, my + dr)

    for dr, dc in order:

        @pl.when(inside(dr, dc))
        def _():
            halo(dr, dc).start()

    near[4] = msg[...]
    for dr, dc in order:

        @pl.when(inside(dr, dc))
        def _():
            copy = halo(dr, dc)
            copy.wait_send()
            pltpu.make_async_remote_copy(
                src_ref=msg, dst_ref=near.at[(dr + 1) * 3 + dc + 1],
                send_sem=n_send.at[(dr + 1) * 3 + dc + 1], recv_sem=n_recv.at[(dr + 1) * 3 + dc + 1],
                device_id=(me + dc, my + dr), device_id_type=MESH,
            ).wait_recv()

    around = [near[i].astype(F32)[0:8] for i in range(9)]
    taps = 9 * chan
    wide_taps, rest_taps = [], []
    for i in range(2):
        for j in range(2):
            parts = [jnp.zeros((8, LANES), F32), jnp.zeros((8, LANES), F32)]
            for v in range(3):
                for u in range(3):
                    ri, ci = i + v - 1, j + u - 1
                    at = (ri // 2 + 1) * 3 + ci // 2 + 1
                    src = ((ri % 2) * 2 + ci % 2) * chan
                    to = (v * 3 + u) * chan
                    shift = (to - src) % LANES
                    cell = pltpu.roll(around[at], shift, 1) if shift else around[at]
                    inner_at = to % LANES
                    parts[to // LANES] = jnp.where(
                        (lane8 >= inner_at) & (lane8 < inner_at + chan), cell, parts[to // LANES]
                    )
            wide_taps.append(parts[0])
            rest_taps.append(parts[1])
    wide_taps = jnp.concatenate(wide_taps, axis=0).astype(BF16)
    rest_taps = jnp.concatenate(rest_taps, axis=0).astype(BF16)[:, : taps - LANES]
    steps = []
    for u in range(3):
        steps.append(
            jnp.dot(wide_taps, cw[pl.ds(u * taps, LANES), :], preferred_element_type=F32)
            + jnp.dot(rest_taps, cw[pl.ds(u * taps + LANES, taps - LANES), :], preferred_element_type=F32)
        )
    for copy in pending:
        copy.wait_send()
    gain = gain_ref[...][None, :]
    decoded = []
    for cell in range(4):
        rows = slice(cell * 8, cell * 8 + 8)
        conv = steps[0][rows] + pltpu.roll(steps[1][rows], 7, 0) + pltpu.roll(steps[2][rows], 6, 0)
        square = jnp.sum(conv * conv, axis=1, keepdims=True) / conv.shape[1]
        scaled = conv * lax.rsqrt(square + 1e-6) * gain
        decoded.append(scaled / (1.0 + jnp.exp(-scaled)))
    for f in range(z.frames):
        for i in range(2):
            pair_of = [decoded[i * 2 + j][f : f + 1] for j in range(2)]
            dec_ref[f, i] = jnp.concatenate(pair_of, axis=0).astype(BF16)


def local(
    mesh, stream, queries, span_k, span_v, cache_k, cache_v, cache_age, history, out_weight,
    attn_gate, head_shift, head_scale, head_weight, latent_cache, conv_weight, rms_gain,
):
    queries, span_k, span_v = (t[:, :, 0] for t in (queries, span_k, span_v))
    out_weight, head_weight = out_weight.T, head_weight.T
    z = Sizes(mesh, queries, cache_k, out_weight)
    model, chan = z.model, conv_weight.shape[1]
    vmem = pl.BlockSpec(memory_space=pltpu.VMEM)
    hbm = pl.BlockSpec(memory_space=pl.ANY)
    half = z.all // 2
    dma = lambda *shape: pltpu.SemaphoreType.DMA(shape)
    out, dec = pl.pallas_call(
        functools.partial(kernel, z),
        out_shape=(
            jax.ShapeDtypeStruct((z.frames, model), BF16),
            jax.ShapeDtypeStruct((z.frames, 2, 2, chan), BF16),
        ),
        in_specs=[vmem] * 4 + [pl.BlockSpec(memory_space=pltpu.SMEM)] + [vmem] * 6 + [hbm] * 5,
        out_specs=(vmem, vmem),
        scratch_shapes=[
            pltpu.VMEM((z.all, z.lanes), BF16),
            pltpu.VMEM((z.all, z.lanes), BF16),
            pltpu.VMEM((z.chunks, z.all, z.wide + LANES), BF16),
            pltpu.VMEM((z.chunks, half, z.wide + LANES), BF16),
            pltpu.VMEM((z.chunks, half, z.wide + LANES), BF16),
            pltpu.VMEM((z.chunks, half, z.wide + LANES), BF16),
            pltpu.VMEM((z.halves * z.keys, z.lanes), BF16),
            pltpu.VMEM((z.halves * z.keys, z.lanes), BF16),
            pltpu.VMEM(out_weight.shape, BF16),
            pltpu.VMEM(head_weight.shape, BF16),
            pltpu.VMEM(conv_weight.shape, BF16),
            pltpu.VMEM((z.nhd, z.nsp * z.message, LANES), BF16),
            pltpu.VMEM((z.nhd, z.nsp * z.message, LANES), BF16),
            pltpu.VMEM((z.nsp * z.message, LANES), BF16),
            pltpu.VMEM((z.nsp * z.message, LANES), BF16),
            pltpu.VMEM((9, 16, LANES), BF16),
            pltpu.VMEM((16, LANES), BF16),
            pltpu.VMEM((16, LANES), F32),
            pltpu.VMEM((z.nsp * z.message, z.pieces * z.nsp * z.tp), BF16),
            pltpu.VMEM((z.pieces * z.nsp * 8, z.nsp * z.message), BF16),
            pltpu.VMEM((z.nsp * z.tp, z.part), F32),
            dma(2 * z.halves + 3),
            dma(2, z.nchip), dma(2, z.nchip), dma(2, z.nchip), dma(2, z.nchip), dma(2, 2), dma(2, 2),
            dma(z.chunks), dma(z.chunks),
            dma(z.chunks, z.nchip), dma(z.chunks, z.nchip),
            dma(z.nhd), dma(z.nhd),
            dma(z.nsp), dma(z.nsp),
            dma(9), dma(9),
        ],
        compiler_params=pltpu.CompilerParams(
            collective_id=0, has_side_effects=True, vmem_limit_bytes=56 * 1024 * 1024
        ),
        name="span_block",
    )(
        queries, span_k, span_v, cache_age, history, stream.reshape(z.frames, model),
        attn_gate[None], head_shift[None], head_scale[None], latent_cache, rms_gain,
        cache_k, cache_v, out_weight, head_weight, conv_weight,
    )
    return out.reshape(stream.shape), dec


def solution(mesh):
    placed = (
        P(None, "hd", "sp", None),
        P(None, None, "sp", "hd"),
        P(None, None, "sp", "hd"),
        P(None, None, "sp", "hd"),
        P("sp", "hd"),
        P("sp", "hd"),
        P("sp"),
        P(),
        P("hd", "sp"),
        P(),
        P(),
        P(),
        P(),
        P(None, "hd", "sp", None),
        P(),
        P(),
    )
    return jax.shard_map(
        functools.partial(local, mesh),
        mesh=mesh,
        in_specs=placed,
        out_specs=(P(None, "hd", "sp", None), P(None, "hd", "sp", None)),
        check_vma=False,
    )
```

```python
import functools
import math

import jax
import jax.numpy as jnp
from jax import lax
from jax.experimental import pallas as pl
from jax.experimental.pallas import tpu as pltpu
from jax.sharding import PartitionSpec as P

HDIM = 128
LANES = 128
MESH = pl.DeviceIdType.MESH
F32 = jnp.float32
BF16 = jnp.bfloat16


def up(value, unit):
    return -(-value // unit) * unit


class Sizes:
    def __init__(self, mesh, queries, cache_k, out_weight):
        self.nsp, self.nhd = mesh.shape["sp"], mesh.shape["hd"]
        self.nchip = self.nsp // 2
        self.frames, self.rows, self.width = queries.shape
        self.heads = self.width // HDIM
        self.own = self.rows // self.nhd
        self.tokens = self.frames * self.rows
        self.slot = up(self.own * self.frames, 4)
        self.tp = self.slot * self.nhd
        self.halves = 2 if self.tp % 16 and self.heads % 2 == 0 else 1
        if self.halves == 1:
            self.tp = up(self.tp, 16)
        self.block = self.halves * self.tp
        self.lanes = self.width // self.halves
        self.pairs = self.heads // self.halves
        self.chunks = 1 if self.pairs % 2 else 2
        self.chunk_pairs = self.pairs // self.chunks
        self.wide = self.lanes // self.chunks
        self.cache = cache_k.shape[0]
        self.keys = up(self.cache + up(self.tp, 16), LANES)
        self.span = self.keys - self.cache
        self.all = self.nsp * self.block
        self.part = out_weight.shape[0]
        self.pieces = -(-self.part // LANES)
        self.message = up(self.pieces * self.slot, 16)
        self.model = self.part * self.nsp

    def slots(self):
        for f in range(self.frames):
            for r in range(self.rows):
                yield (r // self.own) * self.slot + (r % self.own) * self.frames + f, f, r


def div(value, by):
    return value >> (by.bit_length() - 1) if by & (by - 1) == 0 else value // by


def mod(value, by):
    return value & (by - 1) if by & (by - 1) == 0 else value % by


def iota(shape, dim):
    return lax.broadcasted_iota(jnp.int32, shape, dim)


def merge_stats(stats):
    top = functools.reduce(jnp.maximum, stats)
    scales = [jnp.exp(s - top) for s in stats]
    total = functools.reduce(
        jnp.add, [s * pltpu.roll(a, 64, 1) for s, a in zip(stats, scales)]
    )
    return top, total, scales


def kernel(
    z, history_ref, q_hbm, k_hbm, v_hbm, age_hbm, stream_hbm, gate_hbm, shift_hbm, scale_hbm, latc_hbm, gain_hbm,
    ck_hbm, cv_hbm, w_hbm, hw_hbm, cw_hbm,
    so_hbm, dec_hbm,
    q_ref, k_ref, v_ref, age_ref, stream_ref, gate_ref, shift_ref, scale_ref, latc_ref, gain_ref, so_ref, dec_ref,
    g, att, o, o_in, co, o_got, k2, v2, w, hw, cw, zs, z_got, h, r_got, near, msg, tmp, pick_out, pick_in, projected,
    local_sem, z_send, z_recv, x_send, x_recv, c_send, c_recv, sib_send, sib_recv, b_send, b_recv,
    hd_send, hd_recv, e_send, e_recv, n_send, n_recv,
):
    me, my = lax.axis_index("sp"), lax.axis_index("hd")
    core, chip = me % 2, me // 2
    sib = me + 1 - 2 * core
    nchip, block = z.nchip, z.block

    far, side = nchip // 2, chip % 2

    def place(which_chip):
        return (which_chip % 2) * far + which_chip // 2

    def rows_of(which_core, which_chip):
        return pl.ds(pl.multiple_of((which_core * nchip + place(which_chip)) * block, block), block)

    def chip_rows(which_chip):
        return pl.ds(pl.multiple_of(place(which_chip) * block, block), block)

    def remote(src, dst, ssem, rsem, sp, hd):
        return pltpu.make_async_remote_copy(
            src_ref=src, dst_ref=dst, send_sem=ssem, recv_sem=rsem,
            device_id=(sp, hd), device_id_type=MESH,
        )

    def packed(ref):
        row = iota((z.tp, z.width), 0)
        out = jnp.zeros((z.tp, z.width), F32)
        for slot, f, r in z.slots():
            out = jnp.where(row == slot, ref[f, r : r + 1, :].astype(F32), out)
        return [out[:, i * z.lanes : (i + 1) * z.lanes] for i in range(z.halves)]

    near[...] = jnp.zeros_like(near)

    barrier = pltpu.get_barrier_semaphore()
    for k in range(1, z.nsp):
        pl.semaphore_signal(barrier, inc=1, device_id=((me + k) % z.nsp, my), device_id_type=MESH)
    for k in range(1, z.nhd):
        pl.semaphore_signal(barrier, inc=1, device_id=(me, (my + k) % z.nhd), device_id_type=MESH)

    def inside(dr, dc):
        ok = None
        for step, at, count in ((dr, my, z.nhd), (dc, me, z.nsp)):
            if step:
                here = (at + step >= 0) & (at + step < count)
                ok = here if ok is None else ok & here
        return ok

    greeted = z.nsp - 1 + z.nhd - 1
    for dr in (-1, 1):
        for dc in (-1, 1):

            @pl.when(inside(dr, dc))
            def _():
                pl.semaphore_signal(barrier, inc=1, device_id=(me + dc, my + dr), device_id_type=MESH)

            greeted = greeted + inside(dr, dc).astype(jnp.int32)
    loads = []

    def load(src, dst):
        copy = pltpu.make_async_copy(src, dst, local_sem.at[len(loads)])
        copy.start()
        loads.append(copy)

    load(q_hbm, q_ref)
    load(k_hbm, k_ref)
    load(v_hbm, v_ref)
    load(age_hbm, age_ref)
    for half in range(z.halves):
        cols = pl.ds(half * z.lanes, z.lanes)
        load(ck_hbm.at[:, cols], k2.at[pl.ds(half * z.keys, z.cache)])
        load(cv_hbm.at[:, cols], v2.at[pl.ds(half * z.keys, z.cache)])
    attention_loads = len(loads)
    load(w_hbm, w)
    load(hw_hbm, hw)
    load(cw_hbm, cw)
    for src, dst in (
        (stream_hbm, stream_ref), (gate_hbm, gate_ref), (shift_hbm, shift_ref), (scale_hbm, scale_ref),
        (latc_hbm, latc_ref), (gain_hbm, gain_ref),
    ):
        load(src, dst)
    loads[0].wait()

    mine_q = jnp.concatenate(packed(q_ref), axis=0).astype(BF16)
    g[rows_of(core, chip), :] = mine_q
    pl.semaphore_wait(barrier, greeted)

    partner = (chip + 1 - 2 * side) * 2 + core
    pending = []

    def distant(k):
        return (chip // 2 + far - k) % far

    def pass_on(buf, phase, rows, sems, slot, to):
        ssem, rsem = sems
        copy = remote(buf.at[rows], buf.at[rows], ssem.at[phase, slot], rsem.at[phase, slot], to, my)
        copy.start()
        pending.append(copy)
        return copy

    along, across, within = (z_send, z_recv), (x_send, x_recv), (c_send, c_recv)

    class Gather:
        def __init__(self, buf, phase):
            self.at = (buf, phase)
            mine = rows_of(core, chip)
            self.z = [
                pass_on(*self.at, mine, along, k, (((chip // 2 + k) % far) * 2 + side) * 2 + core)
                for k in range(1, far)
            ]
            self.x = [pass_on(*self.at, mine, across, 0, partner)]
            self.c = []

        def batch(self, which_side):
            rows = pl.ds(pl.multiple_of((core * 2 + which_side) * far * block, far * block), far * block)
            self.c.append(pass_on(*self.at, rows, within, len(self.c), sib))

        def relay(self):
            for k in range(1, far):
                self.z[k - 1].wait_recv()
                self.x.append(pass_on(*self.at, rows_of(core, distant(k) * 2 + side), across, k, partner))
            self.batch(side)
            for copy in self.x:
                copy.wait_recv()
            self.batch(1 - side)

        def finish(self):
            for copy in self.c:
                copy.wait_recv()

    asked = Gather(g, 0)
    for copy in loads[1:4]:
        copy.wait()
    for ref, buf in ((k_ref, k2), (v_ref, v2)):
        for half, part in enumerate(packed(ref)):
            if z.span > z.tp:
                part = jnp.concatenate([part, jnp.zeros((z.span - z.tp, z.lanes), F32)], axis=0)
            buf[pl.ds(half * z.keys + z.cache, z.span), :] = part.astype(BF16)
    out_rows, in_rows = z.nsp * z.message, z.nsp * z.tp
    out_at, in_at = iota((out_rows, in_rows), 0), iota((out_rows, in_rows), 1)
    out_sp, inner = div(out_at, z.message), mod(out_at, z.message)
    at_chip = mod(out_sp, 2) * nchip + mod(div(out_sp, 2), 2) * far + div(out_sp, 4)
    wanted = in_at == at_chip * z.tp + mod(inner, z.slot)
    for piece in range(z.pieces):
        picked = jnp.where(wanted & (div(inner, z.slot) == piece), 1.0, 0.0).astype(BF16)
        pick_out[:, pl.ds(piece * in_rows, in_rows)] = picked
    to_rows, from_rows = z.nsp * 8, z.nsp * z.message
    to_at, from_at = iota((to_rows, from_rows), 0), iota((to_rows, from_rows), 1)
    to_slot = mod(to_at, 8)
    wanted = from_at - div(to_at, 8) * z.message - to_slot
    for piece in range(z.pieces):
        picked = (wanted == piece * z.slot) & (to_slot < z.slot)
        pick_in[pl.ds(piece * to_rows, to_rows), :] = jnp.where(picked, 1.0, 0.0).astype(BF16)

    half_rows = nchip * block
    chunk = min(half_rows, 256)
    total_keys = z.halves * z.keys
    lane = iota((chunk, LANES), 1)
    scale = 1.0 / math.sqrt(HDIM)
    key = iota((1, z.keys), 1)
    live = jnp.where(age_ref[...][None, :] < history_ref[0], 1.0, 0.0).astype(F32)
    live = jnp.concatenate([live, jnp.zeros((1, z.span), F32)], axis=1)
    for slot, _, _ in z.slots():
        live = jnp.where(key == z.cache + slot, 1.0, live)
    bounds = [jnp.broadcast_to(live, (chunk, z.keys))] * z.halves
    if z.halves > 1:
        row_half = mod(div(iota((chunk, z.keys), 0), z.tp), z.halves)
        bounds = [jnp.where(row_half == half, b, 0.0) for half, b in enumerate(bounds)]
    mask = jnp.concatenate(bounds, axis=1) > 0.0
    ones = jnp.ones((total_keys, LANES), BF16)

    for copy in loads[4:attention_loads]:
        copy.wait()
    asked.relay()

    def attend(which_core, ch):
        def step(at, carry):
            rows = pl.ds(pl.multiple_of(which_core * half_rows + at * chunk, chunk), chunk)
            stats = jnp.zeros((chunk, LANES), F32)
            outs = []
            for j in range(z.chunk_pairs):
                cols = pl.ds(ch * z.wide + j * HDIM, HDIM)
                scores = lax.dot_general(
                    g[rows, cols], k2[:, cols], (((1,), (1,)), ((), ())), preferred_element_type=F32
                )
                scores = jnp.where(mask, scores * scale, -1e30)
                top = jnp.max(scores, axis=1, keepdims=True).astype(BF16).astype(F32)
                weights = jnp.exp(scores - top).astype(BF16)
                out = jnp.dot(
                    weights, jnp.concatenate([v2[:, cols], ones], axis=1), preferred_element_type=F32
                )
                outs.append(out[:, :HDIM].astype(BF16))
                stats = jnp.where(lane == j, top, jnp.where(lane == j + 64, out[:, HDIM:], stats))
            o[ch, rows, :] = jnp.concatenate(outs + [stats.astype(BF16)], axis=1)
            return carry

        if half_rows == chunk:
            step(0, 0)
        else:
            lax.fori_loop(0, half_rows // chunk, step, 0)

    theirs = pl.ds(pl.multiple_of((1 - core) * half_rows, half_rows), half_rows)
    low = iota((block, LANES), 1) < 64

    def give(ch):
        copy = remote(o.at[ch, theirs], o_in.at[ch], sib_send.at[ch], sib_recv.at[ch], sib, my)
        copy.start()
        pending.append(copy)
        return copy

    def merge(ch, given):
        given.wait_recv()
        stat_cols = pl.ds(z.wide, LANES)
        group = far * block
        group_low = iota((group, LANES), 1) < 64
        copies = []
        for across_side in (1, 0):
            to_side = (side + across_side) % 2
            rows = pl.ds(pl.multiple_of(to_side * group, group), group)
            mine = pl.ds(pl.multiple_of(core * half_rows + to_side * group, group), group)
            top, total, (a, b) = merge_stats(
                [o[ch, mine, stat_cols].astype(F32), o_in[ch, rows, stat_cols].astype(F32)]
            )
            merged = []
            for j in range(z.chunk_pairs):
                cols = pl.ds(j * HDIM, HDIM)
                value = (
                    o[ch, mine, cols].astype(F32) * a[:, j : j + 1]
                    + o_in[ch, rows, cols].astype(F32) * b[:, j : j + 1]
                )
                merged.append(value.astype(BF16))
            merged.append(jnp.where(group_low, top, total).astype(BF16))
            co[ch, rows, :] = jnp.concatenate(merged, axis=1)
            for k in range(far):
                if k == 0 and across_side == 0:
                    continue
                to = ((chip // 2 + k) % far) * 2 + to_side
                slot = across_side * far + k
                copy = remote(co.at[ch, chip_rows(to)], o_got.at[ch, chip_rows(chip)],
                              b_send.at[ch, slot], b_recv.at[ch, slot], to * 2 + core, my)
                copy.start()
                copies.append(copy)
        o_got[ch, chip_rows(chip), :] = co[ch, chip_rows(chip), :]
        pending.extend(copies)
        return copies

    def settle(ch, copies):
        for copy in copies:
            copy.wait_recv()
        parts = [pl.ds(i * block, block) for i in range(nchip)]
        top, total, scales = merge_stats([o_got[ch, p, pl.ds(z.wide, LANES)].astype(F32) for p in parts])
        done = []
        inverse = pltpu.roll(1.0 / jnp.where(low, 1.0, total), 64, 1)
        for j in range(z.chunk_pairs):
            cols = pl.ds(j * HDIM, HDIM)
            terms = [o_got[ch, p, cols].astype(F32) * s[:, j : j + 1] for p, s in zip(parts, scales)]
            summed = functools.reduce(jnp.add, terms)
            done.append((summed * inverse[:, j : j + 1]).astype(BF16))
        att[rows_of(core, chip), pl.ds(ch * z.wide, z.wide)] = jnp.concatenate(done, axis=1)

    for ch in range(z.chunks):
        attend(core, ch)
    asked.finish()
    given = []
    for ch in range(z.chunks):
        attend(1 - core, ch)
        given.append(give(ch))
    partials = [merge(ch, given[ch]) for ch in range(z.chunks)]
    for ch in range(z.chunks):
        settle(ch, partials[ch])
    shared = Gather(att, 1)

    def project(which_core):
        part_rows = nchip * z.tp
        tokens = att[pl.ds(pl.multiple_of(which_core * half_rows, half_rows), half_rows), :]
        total = None
        for half in range(z.halves):
            term = lax.dot_general(
                tokens, w[:, pl.ds(half * z.lanes, z.lanes)], (((1,), (1,)), ((), ())),
                preferred_element_type=F32,
            )
            term = term.reshape(nchip, z.halves, z.tp, z.part)[:, half]
            total = term if total is None else total + term
        rows = pl.ds(pl.multiple_of(which_core * part_rows, part_rows), part_rows)
        projected[rows, :] = total.reshape(part_rows, z.part)

    for copy in loads[attention_loads:]:
        copy.wait()
    shared.relay()
    project(core)
    shared.finish()
    project(1 - core)
    proj = projected[...]
    wide = z.pieces * LANES
    if wide > z.part:
        proj = jnp.concatenate([proj, jnp.zeros((in_rows, wide - z.part), F32)], axis=1)
    owned = []
    for owner in range(z.nhd):
        turned = pltpu.roll(proj, in_rows - owner * z.slot, 0) if owner else proj
        turned = turned.astype(BF16)
        owned.append(
            jnp.concatenate([turned[:, i * LANES : (i + 1) * LANES] for i in range(z.pieces)], axis=0)
        )
    moved = jnp.dot(pick_out[...], jnp.concatenate(owned, axis=1), preferred_element_type=F32).astype(BF16)
    for owner in range(z.nhd):
        zs[owner] = moved[:, owner * LANES : (owner + 1) * LANES]

    swaps = []
    for k in range(1, z.nhd):
        to = (my + k) % z.nhd
        copy = remote(zs.at[to], z_got.at[my], hd_send.at[k], hd_recv.at[k], me, to)
        copy.start()
        swaps.append(copy)
    summed = zs[my].astype(F32)
    for k in range(1, z.nhd):
        swaps[k - 1].wait_recv()
        summed = summed + z_got[(my + z.nhd - k) % z.nhd].astype(F32)
    h[...] = summed.astype(BF16)

    def message_rows(at):
        return pl.ds(pl.multiple_of(at * z.message, z.message), z.message)

    spread = []
    for k in range(1, z.nsp):
        to = (me + k) % z.nsp
        copy = remote(h.at[message_rows(to)], r_got.at[message_rows(me)], e_send.at[k], e_recv.at[k], to, my)
        copy.start()
        spread.append(copy)
    r_got[message_rows(me), :] = h[message_rows(me), :]
    pending.extend(swaps)
    pending.extend(spread)
    for copy in spread:
        copy.wait_recv()

    picked = jnp.dot(pick_in[...], r_got[...], preferred_element_type=F32)
    by_piece = [picked[i * to_rows : (i + 1) * to_rows] for i in range(z.pieces)]
    lane8 = iota((8, LANES), 1)
    row8 = iota((8, LANES), 0)
    tiles = []
    for tile in range(z.model // LANES):
        value = jnp.zeros((8, LANES), F32)
        begin = tile * LANES
        for s in range(begin // z.part, (begin + LANES - 1) // z.part + 1):
            for piece in range(z.pieces):
                low_at = s * z.part + piece * LANES
                high_at = min(low_at + LANES, (s + 1) * z.part)
                a, b = max(low_at, begin), min(high_at, begin + LANES)
                if a >= b:
                    continue
                cell = by_piece[piece][s * 8 : (s + 1) * 8]
                if (low_at - begin) % LANES:
                    cell = pltpu.roll(cell, (low_at - begin) % LANES, 1)
                value = jnp.where((lane8 >= a - begin) & (lane8 < b - begin), cell, value)
        cols = pl.ds(begin, LANES)
        base_value = jnp.zeros((8, LANES), F32)
        for f in range(z.frames):
            base_value = jnp.where(row8 == f, stream_ref[f : f + 1, cols].astype(F32), base_value)
        value = base_value + gate_ref[:, cols] * value
        rounded = value.astype(BF16)
        so_ref[:, cols] = rounded[: z.frames]
        value = rounded.astype(F32)
        tiles.append(value)
    mean = jnp.sum(functools.reduce(jnp.add, tiles), axis=1, keepdims=True) / z.model
    centred = [t - mean for t in tiles]
    variance = jnp.sum(functools.reduce(jnp.add, [t * t for t in centred]), axis=1, keepdims=True) / z.model
    root = lax.rsqrt(variance + 1e-6)
    normed = []
    for tile, t in enumerate(centred):
        cols = pl.ds(tile * LANES, LANES)
        normed.append(t * root * (1.0 + scale_ref[:, cols]) + shift_ref[:, cols])
    normed = jnp.concatenate(normed, axis=1)
    normed = jnp.concatenate([normed, jnp.zeros_like(normed)], axis=0).astype(BF16)
    patch = lax.dot_general(
        normed, hw[...], (((1,), (1,)), ((), ())), preferred_element_type=F32
    )
    cells = patch.shape[1]
    past = latc_ref.shape[0]
    tmp[...] = jnp.zeros_like(tmp)
    chan = cells // 4
    for f in range(past):
        for a in range(2):
            for b in range(2):
                at = (a * 2 + b) * chan
                tmp[f : f + 1, at : at + chan] = latc_ref[f, a, b : b + 1, :].astype(F32)
    tmp[past : past + z.frames, 0:cells] = patch[0 : z.frames]
    msg[...] = tmp[...].astype(BF16)

    written = [pltpu.make_async_copy(so_ref, so_hbm, local_sem.at[0])]
    order = [(dr, dc) for dr in (-1, 0, 1) for dc in (-1, 0, 1) if (dr, dc) != (0, 0)]

    def halo(dr, dc):
        at = (dr + 1) * 3 + dc + 1
        return remote(msg, near.at[8 - at], n_send.at[at], n_recv.at[8 - at], me + dc, my + dr)

    for dr, dc in order:

        @pl.when(inside(dr, dc))
        def _():
            halo(dr, dc).start()

    near[4] = msg[...]
    written[0].start()
    for copy in pending:
        copy.wait_send()
    for dr, dc in order:

        @pl.when(inside(dr, dc))
        def _():
            copy = halo(dr, dc)
            copy.wait_send()
            pltpu.make_async_remote_copy(
                src_ref=msg, dst_ref=near.at[(dr + 1) * 3 + dc + 1],
                send_sem=n_send.at[(dr + 1) * 3 + dc + 1], recv_sem=n_recv.at[(dr + 1) * 3 + dc + 1],
                device_id=(me + dc, my + dr), device_id_type=MESH,
            ).wait_recv()

    around = [near[i].astype(F32)[0:8] for i in range(9)]
    taps = 9 * chan
    wide_taps, rest_taps = [], []
    for i in range(2):
        for j in range(2):
            parts = [jnp.zeros((8, LANES), F32), jnp.zeros((8, LANES), F32)]
            for v in range(3):
                for u in range(3):
                    ri, ci = i + v - 1, j + u - 1
                    at = (ri // 2 + 1) * 3 + ci // 2 + 1
                    src = ((ri % 2) * 2 + ci % 2) * chan
                    to = (v * 3 + u) * chan
                    shift = (to - src) % LANES
                    cell = pltpu.roll(around[at], shift, 1) if shift else around[at]
                    inner_at = to % LANES
                    parts[to // LANES] = jnp.where(
                        (lane8 >= inner_at) & (lane8 < inner_at + chan), cell, parts[to // LANES]
                    )
            wide_taps.append(parts[0])
            rest_taps.append(parts[1])
    wide_taps = jnp.concatenate(wide_taps, axis=0).astype(BF16)
    rest_taps = jnp.concatenate(rest_taps, axis=0).astype(BF16)[:, : taps - LANES]
    steps = []
    for u in range(3):
        steps.append(
            jnp.dot(wide_taps, cw[pl.ds(u * taps, LANES), :], preferred_element_type=F32)
            + jnp.dot(rest_taps, cw[pl.ds(u * taps + LANES, taps - LANES), :], preferred_element_type=F32)
        )
    gain = gain_ref[...][None, :]
    decoded = []
    for cell in range(4):
        rows = slice(cell * 8, cell * 8 + 8)
        conv = steps[0][rows] + pltpu.roll(steps[1][rows], 7, 0) + pltpu.roll(steps[2][rows], 6, 0)
        square = jnp.sum(conv * conv, axis=1, keepdims=True) / conv.shape[1]
        scaled = conv * lax.rsqrt(square + 1e-6) * gain
        decoded.append(scaled / (1.0 + jnp.exp(-scaled)))
    for f in range(z.frames):
        for i in range(2):
            pair_of = [decoded[i * 2 + j][f : f + 1] for j in range(2)]
            dec_ref[f, i] = jnp.concatenate(pair_of, axis=0).astype(BF16)
    written.append(pltpu.make_async_copy(dec_ref, dec_hbm, local_sem.at[1]))
    written[1].start()
    for copy in written:
        copy.wait()


def hand_over(out_hbm, dec_hbm, so_hbm, do_hbm, sems):
    copies = [
        pltpu.make_async_copy(out_hbm, so_hbm, sems.at[0]),
        pltpu.make_async_copy(dec_hbm, do_hbm, sems.at[1]),
    ]
    for copy in copies:
        copy.start()
    for copy in copies:
        copy.wait()


def local(
    mesh, stream, queries, span_k, span_v, cache_k, cache_v, cache_age, history, out_weight,
    attn_gate, head_shift, head_scale, head_weight, latent_cache, conv_weight, rms_gain,
):
    queries, span_k, span_v = (t[:, :, 0] for t in (queries, span_k, span_v))
    out_weight, head_weight = out_weight.T, head_weight.T
    z = Sizes(mesh, queries, cache_k, out_weight)
    model, chan = z.model, conv_weight.shape[1]
    hbm = pl.BlockSpec(memory_space=pl.ANY)
    half = z.all // 2
    dma = lambda *shape: pltpu.SemaphoreType.DMA(shape)
    shapes = (
        jax.ShapeDtypeStruct((z.frames, model), BF16),
        jax.ShapeDtypeStruct((z.frames, 2, 2, chan), BF16),
    )
    small = (
        queries, span_k, span_v, cache_age, stream.reshape(z.frames, model),
        attn_gate[None], head_shift[None], head_scale[None], latent_cache, rms_gain,
    )
    out, dec = pl.pallas_call(
        functools.partial(kernel, z),
        out_shape=shapes,
        in_specs=[pl.BlockSpec(memory_space=pltpu.SMEM)] + [hbm] * 15,
        out_specs=(hbm, hbm),
        scratch_shapes=[
            *[pltpu.VMEM(t.shape, t.dtype) for t in (*small, *shapes)],
            pltpu.VMEM((z.all, z.lanes), BF16),
            pltpu.VMEM((z.all, z.lanes), BF16),
            pltpu.VMEM((z.chunks, z.all, z.wide + LANES), BF16),
            pltpu.VMEM((z.chunks, half, z.wide + LANES), BF16),
            pltpu.VMEM((z.chunks, half, z.wide + LANES), BF16),
            pltpu.VMEM((z.chunks, half, z.wide + LANES), BF16),
            pltpu.VMEM((z.halves * z.keys, z.lanes), BF16),
            pltpu.VMEM((z.halves * z.keys, z.lanes), BF16),
            pltpu.VMEM(out_weight.shape, BF16),
            pltpu.VMEM(head_weight.shape, BF16),
            pltpu.VMEM(conv_weight.shape, BF16),
            pltpu.VMEM((z.nhd, z.nsp * z.message, LANES), BF16),
            pltpu.VMEM((z.nhd, z.nsp * z.message, LANES), BF16),
            pltpu.VMEM((z.nsp * z.message, LANES), BF16),
            pltpu.VMEM((z.nsp * z.message, LANES), BF16),
            pltpu.VMEM((9, 16, LANES), BF16),
            pltpu.VMEM((16, LANES), BF16),
            pltpu.VMEM((16, LANES), F32),
            pltpu.VMEM((z.nsp * z.message, z.pieces * z.nsp * z.tp), BF16),
            pltpu.VMEM((z.pieces * z.nsp * 8, z.nsp * z.message), BF16),
            pltpu.VMEM((z.nsp * z.tp, z.part), F32),
            dma(2 * z.halves + 13),
            dma(2, z.nchip), dma(2, z.nchip), dma(2, z.nchip), dma(2, z.nchip), dma(2, 2), dma(2, 2),
            dma(z.chunks), dma(z.chunks),
            dma(z.chunks, z.nchip), dma(z.chunks, z.nchip),
            dma(z.nhd), dma(z.nhd),
            dma(z.nsp), dma(z.nsp),
            dma(9), dma(9),
        ],
        compiler_params=pltpu.CompilerParams(
            collective_id=0, has_side_effects=True, vmem_limit_bytes=56 * 1024 * 1024
        ),
        name="span_block",
    )(
        history, *small, cache_k, cache_v, out_weight, head_weight, conv_weight,
    )
    out, dec = pl.pallas_call(
        hand_over,
        out_shape=shapes,
        in_specs=[hbm] * 2,
        out_specs=(hbm, hbm),
        scratch_shapes=[dma(2)],
        compiler_params=pltpu.CompilerParams(vmem_limit_bytes=63 * 1024 * 1024),
        name="hand_over",
    )(out, dec)
    return out.reshape(stream.shape), dec


def solution(mesh):
    placed = (
        P(None, "hd", "sp", None),
        P(None, None, "sp", "hd"),
        P(None, None, "sp", "hd"),
        P(None, None, "sp", "hd"),
        P("sp", "hd"),
        P("sp", "hd"),
        P("sp"),
        P(),
        P("hd", "sp"),
        P(),
        P(),
        P(),
        P(),
        P(None, "hd", "sp", None),
        P(),
        P(),
    )
    return jax.shard_map(
        functools.partial(local, mesh),
        mesh=mesh,
        in_specs=placed,
        out_specs=(P(None, "hd", "sp", None), P(None, "hd", "sp", None)),
        check_vma=False,
    )
```

```python
import functools
import math

import jax
import jax.numpy as jnp
from jax import lax
from jax.experimental import pallas as pl
from jax.experimental.pallas import tpu as pltpu
from jax.sharding import PartitionSpec as P

HDIM = 128
LANES = 128
MESH = pl.DeviceIdType.MESH
F32 = jnp.float32
BF16 = jnp.bfloat16


def up(value, unit):
    return -(-value // unit) * unit


class Sizes:
    def __init__(self, mesh, queries, cache_k, out_weight):
        self.nsp, self.nhd = mesh.shape["sp"], mesh.shape["hd"]
        self.nchip = self.nsp // 2
        self.frames, self.rows, self.width = queries.shape
        self.heads = self.width // HDIM
        self.own = self.rows // self.nhd
        self.tokens = self.frames * self.rows
        self.slot = up(self.own * self.frames, 4)
        self.tp = self.slot * self.nhd
        self.halves = 2 if self.tp % 16 and self.heads % 2 == 0 else 1
        if self.halves == 1:
            self.tp = up(self.tp, 16)
        self.block = self.halves * self.tp
        self.lanes = self.width // self.halves
        self.pairs = self.heads // self.halves
        self.chunks = 1 if self.pairs % 2 else 2
        self.chunk_pairs = self.pairs // self.chunks
        self.wide = self.lanes // self.chunks
        self.cache = cache_k.shape[0]
        self.keys = up(self.cache + up(self.tp, 16), LANES)
        self.span = self.keys - self.cache
        self.all = self.nsp * self.block
        self.part = out_weight.shape[0]
        self.pieces = -(-self.part // LANES)
        self.message = up(self.pieces * self.slot, 16)
        self.model = self.part * self.nsp
        self.direct = self.nsp * self.nhd <= 64

    def slots(self):
        for f in range(self.frames):
            for r in range(self.rows):
                yield (r // self.own) * self.slot + (r % self.own) * self.frames + f, f, r


def div(value, by):
    return value >> (by.bit_length() - 1) if by & (by - 1) == 0 else value // by


def mod(value, by):
    return value & (by - 1) if by & (by - 1) == 0 else value % by


def iota(shape, dim):
    return lax.broadcasted_iota(jnp.int32, shape, dim)


def merge_stats(stats):
    top = functools.reduce(jnp.maximum, stats)
    scales = [jnp.exp(s - top) for s in stats]
    total = functools.reduce(
        jnp.add, [s * pltpu.roll(a, 64, 1) for s, a in zip(stats, scales)]
    )
    return top, total, scales


def kernel(
    z, history_ref, q_hbm, k_hbm, v_hbm, age_hbm, stream_hbm, gate_hbm, shift_hbm, scale_hbm, latc_hbm, gain_hbm,
    ck_hbm, cv_hbm, w_hbm, hw_hbm, cw_hbm,
    so_hbm, dec_hbm,
    q_ref, k_ref, v_ref, age_ref, stream_ref, gate_ref, shift_ref, scale_ref, latc_ref, gain_ref, so_ref, dec_ref,
    g, att, o, o_in, co, o_got, k2, v2, w, hw, cw, zs, z_got, h, r_got, near, msg, tmp, pick_out, pick_in, projected,
    local_sem, z_send, z_recv, x_send, x_recv, c_send, c_recv, sib_send, sib_recv, b_send, b_recv,
    hd_send, hd_recv, e_send, e_recv, n_send, n_recv,
):
    me, my = lax.axis_index("sp"), lax.axis_index("hd")
    core, chip = me % 2, me // 2
    sib = me + 1 - 2 * core
    nchip, block = z.nchip, z.block

    far, side = nchip // 2, chip % 2

    def place(which_chip):
        return (which_chip % 2) * far + which_chip // 2

    def rows_of(which_core, which_chip):
        return pl.ds(pl.multiple_of((which_core * nchip + place(which_chip)) * block, block), block)

    def chip_rows(which_chip):
        return pl.ds(pl.multiple_of(place(which_chip) * block, block), block)

    def remote(src, dst, ssem, rsem, sp, hd):
        return pltpu.make_async_remote_copy(
            src_ref=src, dst_ref=dst, send_sem=ssem, recv_sem=rsem,
            device_id=(sp, hd), device_id_type=MESH,
        )

    def packed(ref):
        row = iota((z.tp, z.width), 0)
        out = jnp.zeros((z.tp, z.width), F32)
        for slot, f, r in z.slots():
            out = jnp.where(row == slot, ref[f, r : r + 1, :].astype(F32), out)
        return [out[:, i * z.lanes : (i + 1) * z.lanes] for i in range(z.halves)]

    near[...] = jnp.zeros_like(near)

    barrier = pltpu.get_barrier_semaphore()
    if z.direct:
        for k in range(z.nsp, z.nsp * z.nhd):
            there = ((me + k) % z.nsp, (my + k // z.nsp) % z.nhd)
            pl.semaphore_signal(barrier, inc=1, device_id=there, device_id_type=MESH)
    for k in range(1, z.nsp):
        pl.semaphore_signal(barrier, inc=1, device_id=((me + k) % z.nsp, my), device_id_type=MESH)
    for k in range(1, 1 if z.direct else z.nhd):
        pl.semaphore_signal(barrier, inc=1, device_id=(me, (my + k) % z.nhd), device_id_type=MESH)

    def inside(dr, dc):
        ok = None
        for step, at, count in ((dr, my, z.nhd), (dc, me, z.nsp)):
            if step:
                here = (at + step >= 0) & (at + step < count)
                ok = here if ok is None else ok & here
        return ok

    greeted = z.nsp * z.nhd - 1 if z.direct else z.nsp - 1 + z.nhd - 1
    for dr in () if z.direct else (-1, 1):
        for dc in (-1, 1):

            @pl.when(inside(dr, dc))
            def _():
                pl.semaphore_signal(barrier, inc=1, device_id=(me + dc, my + dr), device_id_type=MESH)

            greeted = greeted + inside(dr, dc).astype(jnp.int32)
    loads = []

    def load(src, dst):
        copy = pltpu.make_async_copy(src, dst, local_sem.at[len(loads)])
        copy.start()
        loads.append(copy)

    load(q_hbm, q_ref)
    load(k_hbm, k_ref)
    load(v_hbm, v_ref)
    load(age_hbm, age_ref)
    for half in range(z.halves):
        cols = pl.ds(half * z.lanes, z.lanes)
        load(ck_hbm.at[:, cols], k2.at[pl.ds(half * z.keys, z.cache)])
        load(cv_hbm.at[:, cols], v2.at[pl.ds(half * z.keys, z.cache)])
    attention_loads = len(loads)
    load(w_hbm, w)
    load(hw_hbm, hw)
    load(cw_hbm, cw)
    for src, dst in (
        (stream_hbm, stream_ref), (gate_hbm, gate_ref), (shift_hbm, shift_ref), (scale_hbm, scale_ref),
        (latc_hbm, latc_ref), (gain_hbm, gain_ref),
    ):
        load(src, dst)
    loads[0].wait()

    mine_q = jnp.concatenate(packed(q_ref), axis=0).astype(BF16)
    g[rows_of(core, chip), :] = mine_q
    pl.semaphore_wait(barrier, greeted)

    partner = (chip + 1 - 2 * side) * 2 + core
    pending = []

    def distant(k):
        return (chip // 2 + far - k) % far

    def pass_on(buf, phase, rows, sems, slot, to):
        ssem, rsem = sems
        copy = remote(buf.at[rows], buf.at[rows], ssem.at[phase, slot], rsem.at[phase, slot], to, my)
        copy.start()
        pending.append(copy)
        return copy

    along, across, within = (z_send, z_recv), (x_send, x_recv), (c_send, c_recv)

    class Gather:
        def __init__(self, buf, phase):
            self.at = (buf, phase)
            mine = rows_of(core, chip)
            self.z = [
                pass_on(*self.at, mine, along, k, (((chip // 2 + k) % far) * 2 + side) * 2 + core)
                for k in range(1, far)
            ]
            self.x = [pass_on(*self.at, mine, across, 0, partner)]
            self.c = []

        def batch(self, which_side):
            rows = pl.ds(pl.multiple_of((core * 2 + which_side) * far * block, far * block), far * block)
            self.c.append(pass_on(*self.at, rows, within, len(self.c), sib))

        def relay(self):
            for k in range(1, far):
                self.z[k - 1].wait_recv()
                self.x.append(pass_on(*self.at, rows_of(core, distant(k) * 2 + side), across, k, partner))
            self.batch(side)
            for copy in self.x:
                copy.wait_recv()
            self.batch(1 - side)

        def finish(self):
            for copy in self.c:
                copy.wait_recv()

    asked = Gather(g, 0)
    for copy in loads[1:4]:
        copy.wait()
    for ref, buf in ((k_ref, k2), (v_ref, v2)):
        for half, part in enumerate(packed(ref)):
            if z.span > z.tp:
                part = jnp.concatenate([part, jnp.zeros((z.span - z.tp, z.lanes), F32)], axis=0)
            buf[pl.ds(half * z.keys + z.cache, z.span), :] = part.astype(BF16)
    out_rows, in_rows = z.nsp * z.message, z.nsp * z.tp
    out_at, in_at = iota((out_rows, in_rows), 0), iota((out_rows, in_rows), 1)
    out_sp, inner = div(out_at, z.message), mod(out_at, z.message)
    at_chip = mod(out_sp, 2) * nchip + mod(div(out_sp, 2), 2) * far + div(out_sp, 4)
    wanted = in_at == at_chip * z.tp + mod(inner, z.slot)
    for piece in range(z.pieces):
        picked = jnp.where(wanted & (div(inner, z.slot) == piece), 1.0, 0.0).astype(BF16)
        pick_out[:, pl.ds(piece * in_rows, in_rows)] = picked
    to_rows, from_rows = z.nsp * 8, z.nsp * z.message
    to_at, from_at = iota((to_rows, from_rows), 0), iota((to_rows, from_rows), 1)
    to_slot = mod(to_at, 8)
    wanted = from_at - div(to_at, 8) * z.message - to_slot
    for piece in range(z.pieces):
        picked = (wanted == piece * z.slot) & (to_slot < z.slot)
        pick_in[pl.ds(piece * to_rows, to_rows), :] = jnp.where(picked, 1.0, 0.0).astype(BF16)

    half_rows = nchip * block
    chunk = min(half_rows, 256)
    total_keys = z.halves * z.keys
    lane = iota((chunk, LANES), 1)
    scale = 1.0 / math.sqrt(HDIM)
    key = iota((1, z.keys), 1)
    live = jnp.where(age_ref[...][None, :] < history_ref[0], 1.0, 0.0).astype(F32)
    live = jnp.concatenate([live, jnp.zeros((1, z.span), F32)], axis=1)
    for slot, _, _ in z.slots():
        live = jnp.where(key == z.cache + slot, 1.0, live)
    bounds = [jnp.broadcast_to(live, (chunk, z.keys))] * z.halves
    if z.halves > 1:
        row_half = mod(div(iota((chunk, z.keys), 0), z.tp), z.halves)
        bounds = [jnp.where(row_half == half, b, 0.0) for half, b in enumerate(bounds)]
    mask = jnp.concatenate(bounds, axis=1) > 0.0
    ones = jnp.ones((total_keys, LANES), BF16)

    for copy in loads[4:attention_loads]:
        copy.wait()
    asked.relay()

    def attend(which_core, ch):
        def step(at, carry):
            rows = pl.ds(pl.multiple_of(which_core * half_rows + at * chunk, chunk), chunk)
            stats = jnp.zeros((chunk, LANES), F32)
            outs = []
            for j in range(z.chunk_pairs):
                cols = pl.ds(ch * z.wide + j * HDIM, HDIM)
                scores = lax.dot_general(
                    g[rows, cols], k2[:, cols], (((1,), (1,)), ((), ())), preferred_element_type=F32
                )
                scores = jnp.where(mask, scores * scale, -1e30)
                top = jnp.max(scores, axis=1, keepdims=True).astype(BF16).astype(F32)
                weights = jnp.exp(scores - top).astype(BF16)
                out = jnp.dot(
                    weights, jnp.concatenate([v2[:, cols], ones], axis=1), preferred_element_type=F32
                )
                outs.append(out[:, :HDIM].astype(BF16))
                stats = jnp.where(lane == j, top, jnp.where(lane == j + 64, out[:, HDIM:], stats))
            o[ch, rows, :] = jnp.concatenate(outs + [stats.astype(BF16)], axis=1)
            return carry

        if half_rows == chunk:
            step(0, 0)
        else:
            lax.fori_loop(0, half_rows // chunk, step, 0)

    theirs = pl.ds(pl.multiple_of((1 - core) * half_rows, half_rows), half_rows)
    low = iota((block, LANES), 1) < 64

    def give(ch):
        copy = remote(o.at[ch, theirs], o_in.at[ch], sib_send.at[ch], sib_recv.at[ch], sib, my)
        copy.start()
        pending.append(copy)
        return copy

    def merge(ch, given):
        given.wait_recv()
        stat_cols = pl.ds(z.wide, LANES)
        group = far * block
        group_low = iota((group, LANES), 1) < 64
        copies = []
        for across_side in (1, 0):
            to_side = (side + across_side) % 2
            rows = pl.ds(pl.multiple_of(to_side * group, group), group)
            mine = pl.ds(pl.multiple_of(core * half_rows + to_side * group, group), group)
            top, total, (a, b) = merge_stats(
                [o[ch, mine, stat_cols].astype(F32), o_in[ch, rows, stat_cols].astype(F32)]
            )
            merged = []
            for j in range(z.chunk_pairs):
                cols = pl.ds(j * HDIM, HDIM)
                value = (
                    o[ch, mine, cols].astype(F32) * a[:, j : j + 1]
                    + o_in[ch, rows, cols].astype(F32) * b[:, j : j + 1]
                )
                merged.append(value.astype(BF16))
            merged.append(jnp.where(group_low, top, total).astype(BF16))
            co[ch, rows, :] = jnp.concatenate(merged, axis=1)
            for k in range(far):
                if k == 0 and across_side == 0:
                    continue
                to = ((chip // 2 + k) % far) * 2 + to_side
                slot = across_side * far + k
                copy = remote(co.at[ch, chip_rows(to)], o_got.at[ch, chip_rows(chip)],
                              b_send.at[ch, slot], b_recv.at[ch, slot], to * 2 + core, my)
                copy.start()
                copies.append(copy)
        o_got[ch, chip_rows(chip), :] = co[ch, chip_rows(chip), :]
        pending.extend(copies)
        return copies

    def settle(ch, copies):
        for copy in copies:
            copy.wait_recv()
        parts = [pl.ds(i * block, block) for i in range(nchip)]
        top, total, scales = merge_stats([o_got[ch, p, pl.ds(z.wide, LANES)].astype(F32) for p in parts])
        done = []
        inverse = pltpu.roll(1.0 / jnp.where(low, 1.0, total), 64, 1)
        for j in range(z.chunk_pairs):
            cols = pl.ds(j * HDIM, HDIM)
            terms = [o_got[ch, p, cols].astype(F32) * s[:, j : j + 1] for p, s in zip(parts, scales)]
            summed = functools.reduce(jnp.add, terms)
            done.append((summed * inverse[:, j : j + 1]).astype(BF16))
        att[rows_of(core, chip), pl.ds(ch * z.wide, z.wide)] = jnp.concatenate(done, axis=1)

    for ch in range(z.chunks):
        attend(core, ch)
    asked.finish()
    given = []
    for ch in range(z.chunks):
        attend(1 - core, ch)
        given.append(give(ch))
    partials = [merge(ch, given[ch]) for ch in range(z.chunks)]
    for ch in range(z.chunks):
        settle(ch, partials[ch])
    shared = Gather(att, 1)

    def project(which_core):
        part_rows = nchip * z.tp
        tokens = att[pl.ds(pl.multiple_of(which_core * half_rows, half_rows), half_rows), :]
        total = None
        for half in range(z.halves):
            term = lax.dot_general(
                tokens, w[:, pl.ds(half * z.lanes, z.lanes)], (((1,), (1,)), ((), ())),
                preferred_element_type=F32,
            )
            term = term.reshape(nchip, z.halves, z.tp, z.part)[:, half]
            total = term if total is None else total + term
        rows = pl.ds(pl.multiple_of(which_core * part_rows, part_rows), part_rows)
        projected[rows, :] = total.reshape(part_rows, z.part)

    for copy in loads[attention_loads:]:
        copy.wait()
    shared.relay()
    project(core)
    shared.finish()
    project(1 - core)
    proj = projected[...]
    wide = z.pieces * LANES
    if wide > z.part:
        proj = jnp.concatenate([proj, jnp.zeros((in_rows, wide - z.part), F32)], axis=1)
    owned = []
    for owner in range(z.nhd):
        turned = pltpu.roll(proj, in_rows - owner * z.slot, 0) if owner else proj
        turned = turned.astype(BF16)
        owned.append(
            jnp.concatenate([turned[:, i * LANES : (i + 1) * LANES] for i in range(z.pieces)], axis=0)
        )
    moved = jnp.dot(pick_out[...], jnp.concatenate(owned, axis=1), preferred_element_type=F32).astype(BF16)
    for owner in range(z.nhd):
        zs[owner] = moved[:, owner * LANES : (owner + 1) * LANES]

    def message_rows(at):
        return pl.ds(pl.multiple_of(at * z.message, z.message), z.message)

    if z.direct:
        spread = []
        for dh in range(z.nhd - 1, -1, -1):
            for ds in range(z.nsp):
                if dh or ds:
                    to_hd, to = (my + dh) % z.nhd, (me + ds) % z.nsp
                    slot = dh * z.nsp + ds
                    copy = remote(zs.at[to_hd, message_rows(to)], z_got.at[my, message_rows(me)],
                                  e_send.at[slot], e_recv.at[slot], to, to_hd)
                    copy.start()
                    spread.append(copy)
        z_got[my, message_rows(me), :] = zs[my, message_rows(me), :]
        pending.extend(spread)
        for copy in spread:
            copy.wait_recv()
        summed = functools.reduce(jnp.add, [z_got[i].astype(F32) for i in range(z.nhd)])
        r_got[...] = summed.astype(BF16)
    else:
        swaps = []
        for k in range(1, z.nhd):
            to = (my + k) % z.nhd
            copy = remote(zs.at[to], z_got.at[my], hd_send.at[k], hd_recv.at[k], me, to)
            copy.start()
            swaps.append(copy)
        summed = zs[my].astype(F32)
        for k in range(1, z.nhd):
            swaps[k - 1].wait_recv()
            summed = summed + z_got[(my + z.nhd - k) % z.nhd].astype(F32)
        h[...] = summed.astype(BF16)

        spread = []
        for k in range(1, z.nsp):
            to = (me + k) % z.nsp
            copy = remote(h.at[message_rows(to)], r_got.at[message_rows(me)], e_send.at[k], e_recv.at[k], to, my)
            copy.start()
            spread.append(copy)
        r_got[message_rows(me), :] = h[message_rows(me), :]
        pending.extend(swaps)
        pending.extend(spread)
        for copy in spread:
            copy.wait_recv()

    picked = jnp.dot(pick_in[...], r_got[...], preferred_element_type=F32)
    by_piece = [picked[i * to_rows : (i + 1) * to_rows] for i in range(z.pieces)]
    lane8 = iota((8, LANES), 1)
    row8 = iota((8, LANES), 0)
    tiles = []
    for tile in range(z.model // LANES):
        value = jnp.zeros((8, LANES), F32)
        begin = tile * LANES
        for s in range(begin // z.part, (begin + LANES - 1) // z.part + 1):
            for piece in range(z.pieces):
                low_at = s * z.part + piece * LANES
                high_at = min(low_at + LANES, (s + 1) * z.part)
                a, b = max(low_at, begin), min(high_at, begin + LANES)
                if a >= b:
                    continue
                cell = by_piece[piece][s * 8 : (s + 1) * 8]
                if (low_at - begin) % LANES:
                    cell = pltpu.roll(cell, (low_at - begin) % LANES, 1)
                value = jnp.where((lane8 >= a - begin) & (lane8 < b - begin), cell, value)
        cols = pl.ds(begin, LANES)
        base_value = jnp.zeros((8, LANES), F32)
        for f in range(z.frames):
            base_value = jnp.where(row8 == f, stream_ref[f : f + 1, cols].astype(F32), base_value)
        value = base_value + gate_ref[:, cols] * value
        rounded = value.astype(BF16)
        so_ref[:, cols] = rounded[: z.frames]
        value = rounded.astype(F32)
        tiles.append(value)
    mean = jnp.sum(functools.reduce(jnp.add, tiles), axis=1, keepdims=True) / z.model
    centred = [t - mean for t in tiles]
    variance = jnp.sum(functools.reduce(jnp.add, [t * t for t in centred]), axis=1, keepdims=True) / z.model
    root = lax.rsqrt(variance + 1e-6)
    normed = []
    for tile, t in enumerate(centred):
        cols = pl.ds(tile * LANES, LANES)
        normed.append(t * root * (1.0 + scale_ref[:, cols]) + shift_ref[:, cols])
    normed = jnp.concatenate(normed, axis=1)
    normed = jnp.concatenate([normed, jnp.zeros_like(normed)], axis=0).astype(BF16)
    patch = lax.dot_general(
        normed, hw[...], (((1,), (1,)), ((), ())), preferred_element_type=F32
    )
    cells = patch.shape[1]
    past = latc_ref.shape[0]
    tmp[...] = jnp.zeros_like(tmp)
    chan = cells // 4
    for f in range(past):
        for a in range(2):
            for b in range(2):
                at = (a * 2 + b) * chan
                tmp[f : f + 1, at : at + chan] = latc_ref[f, a, b : b + 1, :].astype(F32)
    tmp[past : past + z.frames, 0:cells] = patch[0 : z.frames]
    msg[...] = tmp[...].astype(BF16)

    written = [pltpu.make_async_copy(so_ref, so_hbm, local_sem.at[0])]
    order = [(dr, dc) for dr in (-1, 0, 1) for dc in (-1, 0, 1) if (dr, dc) != (0, 0)]

    def halo(dr, dc):
        at = (dr + 1) * 3 + dc + 1
        return remote(msg, near.at[8 - at], n_send.at[at], n_recv.at[8 - at], me + dc, my + dr)

    for dr, dc in order:

        @pl.when(inside(dr, dc))
        def _():
            halo(dr, dc).start()

    near[4] = msg[...]
    written[0].start()
    for copy in pending:
        copy.wait_send()
    for dr, dc in order:

        @pl.when(inside(dr, dc))
        def _():
            copy = halo(dr, dc)
            copy.wait_send()
            pltpu.make_async_remote_copy(
                src_ref=msg, dst_ref=near.at[(dr + 1) * 3 + dc + 1],
                send_sem=n_send.at[(dr + 1) * 3 + dc + 1], recv_sem=n_recv.at[(dr + 1) * 3 + dc + 1],
                device_id=(me + dc, my + dr), device_id_type=MESH,
            ).wait_recv()

    around = [near[i].astype(F32)[0:8] for i in range(9)]
    taps = 9 * chan
    wide_taps, rest_taps = [], []
    for i in range(2):
        for j in range(2):
            parts = [jnp.zeros((8, LANES), F32), jnp.zeros((8, LANES), F32)]
            for v in range(3):
                for u in range(3):
                    ri, ci = i + v - 1, j + u - 1
                    at = (ri // 2 + 1) * 3 + ci // 2 + 1
                    src = ((ri % 2) * 2 + ci % 2) * chan
                    to = (v * 3 + u) * chan
                    shift = (to - src) % LANES
                    cell = pltpu.roll(around[at], shift, 1) if shift else around[at]
                    inner_at = to % LANES
                    parts[to // LANES] = jnp.where(
                        (lane8 >= inner_at) & (lane8 < inner_at + chan), cell, parts[to // LANES]
                    )
            wide_taps.append(parts[0])
            rest_taps.append(parts[1])
    wide_taps = jnp.concatenate(wide_taps, axis=0).astype(BF16)
    rest_taps = jnp.concatenate(rest_taps, axis=0).astype(BF16)[:, : taps - LANES]
    steps = []
    for u in range(3):
        steps.append(
            jnp.dot(wide_taps, cw[pl.ds(u * taps, LANES), :], preferred_element_type=F32)
            + jnp.dot(rest_taps, cw[pl.ds(u * taps + LANES, taps - LANES), :], preferred_element_type=F32)
        )
    gain = gain_ref[...][None, :]
    decoded = []
    for cell in range(4):
        rows = slice(cell * 8, cell * 8 + 8)
        conv = steps[0][rows] + pltpu.roll(steps[1][rows], 7, 0) + pltpu.roll(steps[2][rows], 6, 0)
        square = jnp.sum(conv * conv, axis=1, keepdims=True) / conv.shape[1]
        scaled = conv * lax.rsqrt(square + 1e-6) * gain
        decoded.append(scaled / (1.0 + jnp.exp(-scaled)))
    for f in range(z.frames):
        for i in range(2):
            pair_of = [decoded[i * 2 + j][f : f + 1] for j in range(2)]
            dec_ref[f, i] = jnp.concatenate(pair_of, axis=0).astype(BF16)
    written.append(pltpu.make_async_copy(dec_ref, dec_hbm, local_sem.at[1]))
    written[1].start()
    for copy in written:
        copy.wait()


def hand_over(out_hbm, dec_hbm, so_hbm, do_hbm, sems):
    copies = [
        pltpu.make_async_copy(out_hbm, so_hbm, sems.at[0]),
        pltpu.make_async_copy(dec_hbm, do_hbm, sems.at[1]),
    ]
    for copy in copies:
        copy.start()
    for copy in copies:
        copy.wait()


def local(
    mesh, stream, queries, span_k, span_v, cache_k, cache_v, cache_age, history, out_weight,
    attn_gate, head_shift, head_scale, head_weight, latent_cache, conv_weight, rms_gain,
):
    queries, span_k, span_v = (t[:, :, 0] for t in (queries, span_k, span_v))
    out_weight, head_weight = out_weight.T, head_weight.T
    z = Sizes(mesh, queries, cache_k, out_weight)
    model, chan = z.model, conv_weight.shape[1]
    hbm = pl.BlockSpec(memory_space=pl.ANY)
    half = z.all // 2
    spread = z.nsp * z.nhd if z.direct else z.nsp
    dma = lambda *shape: pltpu.SemaphoreType.DMA(shape)
    shapes = (
        jax.ShapeDtypeStruct((z.frames, model), BF16),
        jax.ShapeDtypeStruct((z.frames, 2, 2, chan), BF16),
    )
    small = (
        queries, span_k, span_v, cache_age, stream.reshape(z.frames, model),
        attn_gate[None], head_shift[None], head_scale[None], latent_cache, rms_gain,
    )
    out, dec = pl.pallas_call(
        functools.partial(kernel, z),
        out_shape=shapes,
        in_specs=[pl.BlockSpec(memory_space=pltpu.SMEM)] + [hbm] * 15,
        out_specs=(hbm, hbm),
        scratch_shapes=[
            *[pltpu.VMEM(t.shape, t.dtype) for t in (*small, *shapes)],
            pltpu.VMEM((z.all, z.lanes), BF16),
            pltpu.VMEM((z.all, z.lanes), BF16),
            pltpu.VMEM((z.chunks, z.all, z.wide + LANES), BF16),
            pltpu.VMEM((z.chunks, half, z.wide + LANES), BF16),
            pltpu.VMEM((z.chunks, half, z.wide + LANES), BF16),
            pltpu.VMEM((z.chunks, half, z.wide + LANES), BF16),
            pltpu.VMEM((z.halves * z.keys, z.lanes), BF16),
            pltpu.VMEM((z.halves * z.keys, z.lanes), BF16),
            pltpu.VMEM(out_weight.shape, BF16),
            pltpu.VMEM(head_weight.shape, BF16),
            pltpu.VMEM(conv_weight.shape, BF16),
            pltpu.VMEM((z.nhd, z.nsp * z.message, LANES), BF16),
            pltpu.VMEM((z.nhd, z.nsp * z.message, LANES), BF16),
            pltpu.VMEM((z.nsp * z.message, LANES), BF16),
            pltpu.VMEM((z.nsp * z.message, LANES), BF16),
            pltpu.VMEM((9, 16, LANES), BF16),
            pltpu.VMEM((16, LANES), BF16),
            pltpu.VMEM((16, LANES), F32),
            pltpu.VMEM((z.nsp * z.message, z.pieces * z.nsp * z.tp), BF16),
            pltpu.VMEM((z.pieces * z.nsp * 8, z.nsp * z.message), BF16),
            pltpu.VMEM((z.nsp * z.tp, z.part), F32),
            dma(2 * z.halves + 13),
            dma(2, z.nchip), dma(2, z.nchip), dma(2, z.nchip), dma(2, z.nchip), dma(2, 2), dma(2, 2),
            dma(z.chunks), dma(z.chunks),
            dma(z.chunks, z.nchip), dma(z.chunks, z.nchip),
            dma(z.nhd), dma(z.nhd),
            dma(spread), dma(spread),
            dma(9), dma(9),
        ],
        compiler_params=pltpu.CompilerParams(
            collective_id=0, has_side_effects=True, vmem_limit_bytes=56 * 1024 * 1024
        ),
        name="span_block",
    )(
        history, *small, cache_k, cache_v, out_weight, head_weight, conv_weight,
    )
    out, dec = pl.pallas_call(
        hand_over,
        out_shape=shapes,
        in_specs=[hbm] * 2,
        out_specs=(hbm, hbm),
        scratch_shapes=[dma(2)],
        compiler_params=pltpu.CompilerParams(vmem_limit_bytes=63 * 1024 * 1024),
        name="hand_over",
    )(out, dec)
    return out.reshape(stream.shape), dec


def solution(mesh):
    placed = (
        P(None, "hd", "sp", None),
        P(None, None, "sp", "hd"),
        P(None, None, "sp", "hd"),
        P(None, None, "sp", "hd"),
        P("sp", "hd"),
        P("sp", "hd"),
        P("sp"),
        P(),
        P("hd", "sp"),
        P(),
        P(),
        P(),
        P(),
        P(None, "hd", "sp", None),
        P(),
        P(),
    )
    return jax.shard_map(
        functools.partial(local, mesh),
        mesh=mesh,
        in_specs=placed,
        out_specs=(P(None, "hd", "sp", None), P(None, "hd", "sp", None)),
        check_vma=False,
    )
```
